128 devices in a mesh: point: 8 (over x, core), cent: 16 (over z, y).
Axes of the slice: x: 4, y: 4, z: 4, core: 2. Of those that a mesh axis runs over, the one named last changes fastest.
Arguments:
- points: bfloat16 [262144, 1024], P(('point', 'cent')), may hold values from -200 to 200
- cluster_ids: int32 [262144], P(('point', 'cent')), may hold values from 0 to 31, as said below
- owner_slot: int32 [32], replicated, may hold values from 0 to 31, as said below
- centroids: bfloat16 [32, 256, 1024], P('point', 'cent'), may hold values from -0.8 to 0.8
Outputs:
- new_centroids: bfloat16 [32, 256, 1024], P('point', 'cent')
- centroid_mass: float32 [32, 256], P('point', 'cent')
The draws below stay inside these ranges and needn't reach their ends.
Inputs may be any that keep to these rules, and one draw needn't show every extreme that they name: `cluster_ids`: cluster of each point. Among the 2048 points of one device at most 128 lie in any one level-one cluster, and in every draw, for each index of cent there is one owner (point index) such that each of that owner's 4 clusters receives exactly 128 points from every device with that cent index; every other cluster receives fewer than 128 from each device. Each block row once: a permutation. Cluster c belongs to point index owner_slot[c] // 4.
All inputs are finite; a program needn't handle non-finite values.
Results may differ from the reference program's by a relative error of at most 0.0063.
Values may be sent and summed in bfloat16 or wider, within the bound.
No kernel may reach another device: no remote copies, remote signals or barrier semaphores. Data moves between devices by JAX's collectives and lax.ppermute only.
A program may use at most 128 MiB of HBM per device.

```python
import jax
import jax.numpy as jnp
from jax import lax

D = 1024
K2 = 256
C1_PER = 4
PTS_DEV = 2048
ITERS = 2
C1 = 32
CAP = 128
NPTS = 262144
N_POINT = 8
N_CENT = 16


def cluster_order(key):
    return jax.random.permutation(jax.random.fold_in(key, 11), C1).astype(jnp.int32)


def point_blocks(key):
    devices_all = N_POINT * N_CENT
    hottest = jax.random.randint(jax.random.fold_in(key, 12), (N_CENT,), 0, N_POINT)
    column = jnp.arange(devices_all, dtype=jnp.int32) % N_CENT
    chosen = hottest[column][:, None]
    blocks = jnp.arange(C1, dtype=jnp.int32)[None, :]
    is_hot = blocks // C1_PER == chosen
    others = jnp.where(blocks >= (chosen + 1) * C1_PER, blocks - C1_PER, blocks)
    spread = PTS_DEV - C1_PER * CAP
    floor_count = spread // (C1 - C1_PER)
    leftover = spread - floor_count * (C1 - C1_PER)
    counts = jnp.where(is_hot, CAP, floor_count + (others < leftover).astype(jnp.int32))
    running = jnp.cumsum(counts, axis=1)
    places = jnp.arange(PTS_DEV, dtype=jnp.int32)
    sequence = jnp.sum((running[:, None, :] <= places[None, :, None]).astype(jnp.int32), axis=2)
    shuffle_keys = jax.random.split(jax.random.fold_in(key, 13), devices_all)
    mixed = jax.vmap(lambda each_key, row_values: jax.random.permutation(each_key, row_values))(shuffle_keys, sequence)
    return mixed.reshape(-1).astype(jnp.int32)


def anchor_table(key):
    return jnp.clip(0.1 * jax.random.normal(jax.random.fold_in(key, 14), (C1, K2, D), jnp.float32), -0.8, 0.8)


def draw_owner_slot(key, part):
    ordering = cluster_order(key)
    return ordering


def draw_cluster_ids(key, part):
    blocks = point_blocks(key)
    ordering = cluster_order(key)
    inverse = jnp.zeros((C1,), jnp.int32).at[ordering].set(jnp.arange(C1, dtype=jnp.int32))
    return inverse[blocks]


def draw_centroids(key, part):
    shared = anchor_table(key)
    return shared.astype(jnp.bfloat16)


def draw_points(key, part):
    blocks = point_blocks(key)
    centre_set = anchor_table(key)
    key = jax.random.fold_in(key, 4)
    chosen = jax.random.randint(jax.random.fold_in(key, 1), (NPTS,), 0, K2)
    anchor = centre_set[blocks, chosen]
    values = anchor + jnp.clip(jax.random.normal(jax.random.fold_in(key, 6), (NPTS, D), jnp.float32), -6.0, 6.0)
    return values.astype(jnp.bfloat16)


def setup_inputs(seed: int = 0) -> dict:
    streams_of = jax.random.split(jax.random.key(seed), 5)
    return {
        "points": draw_points(jax.random.fold_in(streams_of[4], 71), 0),
        "cluster_ids": draw_cluster_ids(jax.random.fold_in(streams_of[4], 71), 0),
        "owner_slot": draw_owner_slot(jax.random.fold_in(streams_of[4], 71), 0),
        "centroids": draw_centroids(jax.random.fold_in(streams_of[4], 71), 0),
    }


score_scale = 0.25
prior_weight = 1.0


def block_update(padded, starts, counts, block_id, centers):
    longest = N_POINT * N_CENT * CAP
    members = lax.dynamic_slice_in_dim(padded, starts[block_id], longest, 0)
    present = (jnp.arange(longest, dtype=jnp.int32) < counts[block_id]).astype(jnp.float32)
    squares = jnp.sum(jnp.square(centers.astype(jnp.float32)), axis=1)
    products = jnp.dot(members, centers.T, preferred_element_type=jnp.float32)
    scores = (products - 0.5 * squares[None, :]) * score_scale
    weights = jax.nn.softmax(scores, axis=-1) * present[:, None]
    totals = jnp.dot(weights.astype(jnp.bfloat16).T, members, preferred_element_type=jnp.float32)
    masses = jnp.sum(weights, axis=0)
    updated = (totals + prior_weight * centers.astype(jnp.float32)) / (masses[:, None] + prior_weight)
    return updated.astype(jnp.bfloat16), masses


def reference(points, cluster_ids, owner_slot, centroids):
    block_of = owner_slot[cluster_ids].astype(jnp.int32)
    order = jnp.argsort(block_of, stable=True)
    cluster_table = jnp.arange(C1, dtype=jnp.int32)
    counts = jnp.sum((block_of[:, None] == cluster_table[None, :]).astype(jnp.int32), axis=0).astype(jnp.int32)
    starts = (jnp.cumsum(counts) - counts).astype(jnp.int32)
    padded = jnp.concatenate([points[order], jnp.zeros((N_POINT * N_CENT * CAP, D), jnp.bfloat16)], axis=0)
    current = centroids
    masses = jnp.zeros((C1, K2), jnp.float32)

    def one_block(member_pair):
        return block_update(padded, starts, counts, member_pair[0], member_pair[1])

    for iteration in range(ITERS):
        current, masses = lax.map(one_block, (cluster_table, current))
    return current, masses
```

```python
import functools

import jax
import jax.numpy as jnp
from jax import lax
from jax.experimental import pallas as pl
from jax.experimental.pallas import tpu as pltpu
from jax.sharding import PartitionSpec as P

ITERS = 2
SCORE_SCALE = 0.25
PRIOR_WEIGHT = 1.0
EXTRA = 128
MARK = 1024.0
MARK_LIMIT = 512.0
GROUP = 256
MIB = 1024 * 1024


def target_kernel(capacity, ids_ref, owner_ref, out_ref):
    clusters = owner_ref.shape[0]
    rows = ids_ref.shape[1]
    before = (
        lax.broadcasted_iota(jnp.int32, (GROUP, GROUP), 0)
        < lax.broadcasted_iota(jnp.int32, (GROUP, GROUP), 1)
    ).astype(jnp.float32).astype(jnp.bfloat16)
    table = lax.broadcasted_iota(jnp.int32, (clusters, GROUP), 0)
    base = (owner_ref[...] * capacity).astype(jnp.float32)
    for g in range(rows // GROUP):
        span = pl.ds(g * GROUP, GROUP)
        hit = (table == ids_ref[:, span]).astype(jnp.float32)
        place = jnp.dot(hit.astype(jnp.bfloat16), before, preferred_element_type=jnp.float32)
        out_ref[:, span] = jnp.sum(hit * (place + base), axis=0, keepdims=True).astype(jnp.int32)
        base = base + jnp.sum(hit, axis=1, keepdims=True)


def targets(cluster_ids, owner_slot, capacity):
    rows = cluster_ids.shape[0]
    return pl.pallas_call(
        functools.partial(target_kernel, capacity),
        out_shape=jax.ShapeDtypeStruct((1, rows), jnp.int32),
        name="targets",
    )(cluster_ids.reshape(1, rows), owner_slot.reshape(-1, 1))


def place_kernel(chunk, per_owner, capacity, owners_step, target_ref, points_ref, out_ref):
    rows = points_ref.shape[0]
    first = pl.program_id(0) * owners_step
    for o in range(owners_step):
        start = ((first + o) * per_owner + chunk) * capacity
        slot = lax.broadcasted_iota(jnp.int32, (capacity, rows), 0) + start
        pick = (slot == target_ref[...]).astype(jnp.float32)
        empty = 1.0 - jnp.sum(pick, axis=1, keepdims=True)
        lane = lax.broadcasted_iota(jnp.int32, (capacity, out_ref.shape[2]), 1)
        got = jnp.dot(pick.astype(jnp.bfloat16), points_ref[...], preferred_element_type=jnp.float32)
        out_ref[o] = (got + jnp.where(lane == 0, MARK * empty, 0.0)).astype(jnp.bfloat16)


def place(target, points, chunk, owners, per_owner, capacity):
    rows, width = points.shape
    step = 4
    return pl.pallas_call(
        functools.partial(place_kernel, chunk, per_owner, capacity, step),
        grid=(owners // step,),
        in_specs=[
            pl.BlockSpec((1, rows), lambda i: (0, 0)),
            pl.BlockSpec((rows, width), lambda i: (0, 0)),
        ],
        out_specs=pl.BlockSpec((step, capacity, width), lambda i: (i, 0, 0)),
        out_shape=jax.ShapeDtypeStruct((owners, capacity, width), jnp.bfloat16),
        compiler_params=pltpu.CompilerParams(vmem_limit_bytes=40 * MIB),
        cost_estimate=pl.CostEstimate(
            flops=2 * owners * capacity * rows * width,
            bytes_accessed=2 * width * (rows + owners * capacity),
            transcendentals=0,
        ),
        name="place",
    )(target, points)


def cluster_kernel(block_ref, rows_ref, out_ref, aug, total, mass, bias):
    step = pl.program_id(0)
    cents, width = block_ref.shape

    @pl.when(step == 0)
    def _():
        mu = block_ref[...]
        aug[:cents] = mu
        unit = lax.broadcasted_iota(jnp.int32, (aug.shape[0] - cents, width), 1) == 0
        aug[cents:] = unit.astype(jnp.float32).astype(jnp.bfloat16)
        wide = mu.astype(jnp.float32)
        bias[...] = 0.5 * jnp.sum(wide * wide, axis=1, keepdims=True)
        total[...] = jnp.zeros_like(total)
        mass[...] = jnp.zeros_like(mass)

    x = rows_ref[...].reshape(-1, width)
    raw = lax.dot_general(aug[...], x, (((1,), (1,)), ((), ())), preferred_element_type=jnp.float32)
    score = (raw[:cents] - bias[...]) * SCORE_SCALE
    present = (raw[cents : cents + 1] < MARK_LIMIT).astype(jnp.float32)
    e = jnp.exp(score - jnp.max(score, axis=0, keepdims=True))
    w = e * (present / jnp.sum(e, axis=0, keepdims=True))
    mass[...] += jnp.sum(w, axis=1, keepdims=True)
    total[...] += jnp.dot(w.astype(jnp.bfloat16), x, preferred_element_type=jnp.float32)

    @pl.when(step == pl.num_programs(0) - 1)
    def _():
        out_ref[:, :width] = total[...].astype(jnp.bfloat16)
        m = mass[...]
        hi = m.astype(jnp.bfloat16).astype(jnp.float32)
        mid = (m - hi).astype(jnp.bfloat16).astype(jnp.float32)
        low = m - hi - mid
        lane = lax.broadcasted_iota(jnp.int32, (cents, EXTRA), 1)
        terms = jnp.where(lane == 0, hi, jnp.where(lane == 1, mid, jnp.where(lane == 2, low, 0.0)))
        out_ref[:, width:] = terms.astype(jnp.bfloat16)


def cluster_sums(block, rows):
    cents, width = block.shape
    sources, capacity, _ = rows.shape
    step = 4
    return pl.pallas_call(
        cluster_kernel,
        grid=(sources // step,),
        in_specs=[
            pl.BlockSpec((cents, width), lambda i: (0, 0)),
            pl.BlockSpec((step, capacity, width), lambda i: (i, 0, 0)),
        ],
        out_specs=pl.BlockSpec((cents, width + EXTRA), lambda i: (0, 0)),
        out_shape=jax.ShapeDtypeStruct((cents, width + EXTRA), jnp.bfloat16),
        scratch_shapes=[
            pltpu.VMEM((cents + 16, width), jnp.bfloat16),
            pltpu.VMEM((cents, width), jnp.float32),
            pltpu.VMEM((cents, 1), jnp.float32),
            pltpu.VMEM((cents, 1), jnp.float32),
        ],
        compiler_params=pltpu.CompilerParams(vmem_limit_bytes=40 * MIB),
        cost_estimate=pl.CostEstimate(
            flops=4 * sources * capacity * cents * width,
            bytes_accessed=2 * width * (sources * capacity + 2 * cents),
            transcendentals=sources * capacity * cents,
        ),
        name="cluster_sums",
    )(block, rows)


def update_kernel(parts_ref, mu_ref, copies_ref, mass_ref):
    sources = parts_ref.shape[0]
    rows, width = mu_ref.shape
    total = parts_ref[0].astype(jnp.float32)
    for s in range(1, sources):
        total = total + parts_ref[s].astype(jnp.float32)
    mass = jnp.sum(total[:, width:], axis=1, keepdims=True)
    mu = mu_ref[...].astype(jnp.float32)
    new = ((total[:, :width] + PRIOR_WEIGHT * mu) / (mass + PRIOR_WEIGHT)).astype(jnp.bfloat16)
    for c in range(copies_ref.shape[0]):
        copies_ref[c] = new
    mass_ref[...] = jnp.broadcast_to(mass, mass_ref.shape)


def update(parts, mu, copies):
    rows, width = mu.shape
    return pl.pallas_call(
        update_kernel,
        out_shape=(
            jax.ShapeDtypeStruct((copies, rows, width), jnp.bfloat16),
            jax.ShapeDtypeStruct((rows, 128), jnp.float32),
        ),
        compiler_params=pltpu.CompilerParams(vmem_limit_bytes=16 * MIB),
        cost_estimate=pl.CostEstimate(
            flops=parts.size, bytes_accessed=2 * parts.size + 2 * copies * rows * width, transcendentals=0
        ),
        name="update",
    )(parts, mu)


def exchange(array, axis):
    return lax.all_to_all(array, axis, split_axis=0, concat_axis=0, tiled=True)


def shards(points, cluster_ids, owner_slot, centroids):
    owners = lax.axis_size("point")
    holders = lax.axis_size("cent")
    rows, width = points.shape
    per_owner, held, _ = centroids.shape
    capacity = 2 * rows // owner_slot.shape[0]

    blocks = lax.all_gather(centroids, "cent", axis=1, tiled=True)
    target = targets(cluster_ids, owner_slot, capacity)
    received = [
        exchange(place(target, points, j, owners, per_owner, capacity), "point")
        for j in range(per_owner)
    ]
    new, masses = [], []
    for j in range(per_owner):
        mine, block = centroids[j], blocks[j]
        for iteration in range(ITERS):
            last = iteration == ITERS - 1
            sums = cluster_sums(block, received[j])
            parts = exchange(sums.reshape(holders, held, width + EXTRA), "cent")
            copies, mass = update(parts, mine, 1 if last else holders)
            mine = copies[0]
            if not last:
                block = exchange(copies, "cent").reshape(holders * held, width)
        new.append(mine)
        masses.append(mass[:, 0])
    return jnp.stack(new), jnp.stack(masses)


def solution(mesh):
    return jax.shard_map(
        shards,
        mesh=mesh,
        in_specs=(P(("point", "cent"), None), P(("point", "cent")), P(), P("point", "cent", None)),
        out_specs=(P("point", "cent", None), P("point", "cent")),
        check_vma=False,
    )
```

```python
import functools

import jax
import jax.numpy as jnp
from jax import lax
from jax.experimental import pallas as pl
from jax.experimental.pallas import tpu as pltpu
from jax.sharding import Mesh, PartitionSpec as P

ITERS = 2
SCORE_SCALE = 0.25
PRIOR_WEIGHT = 1.0
EXTRA = 128
MARK = 1024.0
MARK_LIMIT = 512.0
GROUP = 256
CHUNKS = 2
MIB = 1024 * 1024
VMEM = 60 * MIB


def target_kernel(capacity, ids_ref, owner_ref, out_ref):
    clusters = owner_ref.shape[0]
    rows = ids_ref.shape[1]
    before = (
        lax.broadcasted_iota(jnp.int32, (GROUP, GROUP), 0)
        < lax.broadcasted_iota(jnp.int32, (GROUP, GROUP), 1)
    ).astype(jnp.float32).astype(jnp.bfloat16)
    table = lax.broadcasted_iota(jnp.int32, (clusters, GROUP), 0)
    base = (owner_ref[...] * capacity).astype(jnp.float32)
    for g in range(rows // GROUP):
        span = pl.ds(g * GROUP, GROUP)
        hit = (table == ids_ref[:, span]).astype(jnp.float32)
        place = jnp.dot(hit.astype(jnp.bfloat16), before, preferred_element_type=jnp.float32)
        out_ref[:, span] = jnp.sum(hit * (place + base), axis=0, keepdims=True).astype(jnp.int32)
        base = base + jnp.sum(hit, axis=1, keepdims=True)


def targets(cluster_ids, owner_slot, capacity):
    rows = cluster_ids.shape[0]
    return pl.pallas_call(
        functools.partial(target_kernel, capacity),
        out_shape=jax.ShapeDtypeStruct((1, rows), jnp.int32),
        compiler_params=pltpu.CompilerParams(vmem_limit_bytes=VMEM),
        name="targets",
    )(cluster_ids.reshape(1, rows), owner_slot.reshape(-1, 1))


def place_kernel(first_slot, capacity, target_ref, points_ref, out_ref):
    rows = points_ref.shape[0]
    clusters, slots, width = out_ref.shape
    lane = lax.broadcasted_iota(jnp.int32, (slots, width), 1)
    local = lax.broadcasted_iota(jnp.int32, (slots, rows), 0)
    picks = []
    for c in range(clusters):
        start = (pl.program_id(0) * clusters + c) * capacity + first_slot
        picks.append((local + start == target_ref[...]).astype(jnp.float32))
    pick = jnp.concatenate(picks, axis=0)
    got = jnp.dot(pick.astype(jnp.bfloat16), points_ref[...], preferred_element_type=jnp.float32)
    for c in range(clusters):
        empty = 1.0 - jnp.sum(picks[c], axis=1, keepdims=True)
        part = got[c * slots : (c + 1) * slots]
        out_ref[c] = (part + jnp.where(lane == 0, MARK * empty, 0.0)).astype(jnp.bfloat16)


def place(target, points, clusters, capacity, chunk):
    rows, width = points.shape
    slots = capacity // CHUNKS
    step = 512 // slots
    return pl.pallas_call(
        functools.partial(place_kernel, chunk * slots, capacity),
        grid=(clusters // step,),
        in_specs=[
            pl.BlockSpec((1, rows), lambda i: (0, 0)),
            pl.BlockSpec((rows, width), lambda i: (0, 0)),
        ],
        out_specs=pl.BlockSpec((step, slots, width), lambda i: (i, 0, 0)),
        out_shape=jax.ShapeDtypeStruct((clusters, slots, width), jnp.bfloat16),
        compiler_params=pltpu.CompilerParams(vmem_limit_bytes=VMEM),
        cost_estimate=pl.CostEstimate(
            flops=2 * clusters * slots * rows * width,
            bytes_accessed=2 * width * (rows + clusters * slots),
            transcendentals=0,
        ),
        name="place",
    )(target, points)


def sums_kernel(groups, chunks, steps, carried, finish, *refs):
    blocks, refs = refs[:groups], refs[groups:]
    rows, refs = refs[:chunks], refs[chunks:]
    carry, refs = refs[: 2 * carried], refs[2 * carried :]
    outs, (aug, total, mass, bias) = refs[:-4], refs[-4:]
    step = pl.program_id(0)
    held, width = blocks[0].shape
    cents = groups * held

    @pl.when(step == 0)
    def _():
        for g in range(groups):
            mu = blocks[g][...]
            span = pl.ds(g * held, held)
            aug[span] = mu
            wide = mu.astype(jnp.float32)
            bias[span] = 0.5 * jnp.sum(wide * wide, axis=1, keepdims=True)
        unit = lax.broadcasted_iota(jnp.int32, (aug.shape[0] - cents, width), 1) == 0
        aug[cents:] = unit.astype(jnp.float32).astype(jnp.bfloat16)
        if carried:
            total[...] = carry[0][...]
            mass[...] = carry[1][...]
        else:
            total[...] = jnp.zeros_like(total)
            mass[...] = jnp.zeros_like(mass)

    def accumulate(rows_ref):
        x = rows_ref[...].reshape(-1, width)
        raw = lax.dot_general(
            aug[...], x, (((1,), (1,)), ((), ())), preferred_element_type=jnp.float32
        )
        score = (raw[:cents] - bias[...]) * SCORE_SCALE
        present = (raw[cents : cents + 1] < MARK_LIMIT).astype(jnp.float32)
        e = jnp.exp(score - jnp.max(score, axis=0, keepdims=True))
        w = e * (present / jnp.sum(e, axis=0, keepdims=True))
        mass[...] += jnp.sum(w, axis=1, keepdims=True)
        total[...] += jnp.dot(w.astype(jnp.bfloat16), x, preferred_element_type=jnp.float32)

    for c in range(chunks):
        if chunks == 1:
            accumulate(rows[c])
        else:
            pl.when(step // steps == c)(functools.partial(accumulate, rows[c]))

    @pl.when(step == chunks * steps - 1)
    def _():
        if not finish:
            outs[0][...] = total[...]
            outs[1][...] = mass[...]
            return
        lane = lax.broadcasted_iota(jnp.int32, (held, EXTRA), 1)
        for g in range(groups):
            span = pl.ds(g * held, held)
            outs[g][:, :width] = total[span].astype(jnp.bfloat16)
            outs[g][:, width:] = terms(mass[span], lane)


def terms(m, lane):
    hi = m.astype(jnp.bfloat16).astype(jnp.float32)
    mid = (m - hi).astype(jnp.bfloat16).astype(jnp.float32)
    low = m - hi - mid
    parts = jnp.where(lane == 0, hi, jnp.where(lane == 1, mid, jnp.where(lane == 2, low, 0.0)))
    return parts.astype(jnp.bfloat16)


def cluster_sums(blocks, rows, carry=(), finish=True):
    groups, chunks = len(blocks), len(rows)
    held, width = blocks[0].shape
    sources, slots, _ = rows[0].shape
    cents = groups * held
    step = max(1, 512 // slots)
    steps = sources // step

    def whole(shape):
        return pl.BlockSpec(shape, lambda i: (0,) * len(shape))

    def chunk_spec(c):
        return pl.BlockSpec(
            (step, slots, width), lambda i: (jnp.clip(i - c * steps, 0, steps - 1), 0, 0)
        )

    if finish:
        shapes = [jax.ShapeDtypeStruct((held, width + EXTRA), jnp.bfloat16)] * groups
    else:
        shapes = [
            jax.ShapeDtypeStruct((cents, width), jnp.float32),
            jax.ShapeDtypeStruct((cents, 1), jnp.float32),
        ]
    count = chunks * sources * slots
    return pl.pallas_call(
        functools.partial(sums_kernel, groups, chunks, steps, 1 if carry else 0, finish),
        grid=(chunks * steps,),
        in_specs=[whole((held, width))] * groups
        + [chunk_spec(c) for c in range(chunks)]
        + [whole(a.shape) for a in carry],
        out_specs=[whole(s.shape) for s in shapes],
        out_shape=shapes,
        scratch_shapes=[
            pltpu.VMEM((cents + 16, width), jnp.bfloat16),
            pltpu.VMEM((cents, width), jnp.float32),
            pltpu.VMEM((cents, 1), jnp.float32),
            pltpu.VMEM((cents, 1), jnp.float32),
        ],
        compiler_params=pltpu.CompilerParams(vmem_limit_bytes=VMEM),
        cost_estimate=pl.CostEstimate(
            flops=4 * count * cents * width,
            bytes_accessed=2 * width * (count + 2 * cents),
            transcendentals=count * cents,
        ),
        name="cluster_sums",
    )(*blocks, *rows, *carry)


def update_kernel(packed, count, *refs):
    parts, mu_ref, out_ref = refs[:count], refs[count], refs[count + 1]
    rows, width = mu_ref.shape
    total = parts[0][...].astype(jnp.float32)
    for s in range(1, count):
        total = total + parts[s][...].astype(jnp.float32)
    mass = jnp.sum(total[:, width:], axis=1, keepdims=True)
    mu = mu_ref[...].astype(jnp.float32)
    new = (total[:, :width] + PRIOR_WEIGHT * mu) / (mass + PRIOR_WEIGHT)
    out_ref[:, :width] = new.astype(jnp.bfloat16)
    if packed:
        out_ref[:, width:] = terms(mass, lax.broadcasted_iota(jnp.int32, (rows, EXTRA), 1))


def update(parts, mu, packed):
    rows, width = mu.shape
    return pl.pallas_call(
        functools.partial(update_kernel, packed, len(parts)),
        out_shape=jax.ShapeDtypeStruct((rows, width + (EXTRA if packed else 0)), jnp.bfloat16),
        compiler_params=pltpu.CompilerParams(vmem_limit_bytes=VMEM),
        cost_estimate=pl.CostEstimate(
            flops=len(parts) * rows * width,
            bytes_accessed=2 * (len(parts) + 2) * rows * width,
            transcendentals=0,
        ),
        name="update",
    )(*parts, mu)


def exchange(array, axis):
    return lax.all_to_all(array, axis, split_axis=0, concat_axis=0, tiled=True)


def shards(points, cluster_ids, owner_slot, centroids):
    rows, width = points.shape
    clusters = owner_slot.shape[0]
    capacity = 2 * rows // clusters
    per_owner, held, _ = centroids.shape
    ny, nz = lax.axis_size("y"), lax.axis_size("z")
    y = lax.axis_index("y")
    shifts = [[(i, (i + d) % ny) for i in range(ny)] for d in range(ny)]

    spread = jnp.broadcast_to(centroids[:, None], (nz, ny, held, width))
    gathered = exchange(spread.reshape(nz * ny, held, width), ("z", "y"))
    by_y = gathered.reshape(nz, ny, held, width).swapaxes(0, 1).reshape(ny, nz * held, width)
    blocks = [lax.dynamic_index_in_dim(by_y, (y + d) % ny, 0, keepdims=False) for d in range(ny)]
    mine = blocks[0]

    target = targets(cluster_ids, owner_slot, capacity)
    received = [
        exchange(place(target, points, clusters, capacity, c), ("x", "core", "z"))
        for c in range(CHUNKS)
    ]
    for iteration in range(ITERS):
        last = iteration == ITERS - 1
        if iteration == 0:
            carry = ()
            for c in range(CHUNKS - 1):
                carry = cluster_sums(blocks, received[c : c + 1], carry, finish=False)
            sums = cluster_sums(blocks, received[CHUNKS - 1 :], carry)
        else:
            sums = cluster_sums(blocks, received)
        parts = [sums[0]] + [lax.ppermute(sums[d], "y", shifts[d]) for d in range(1, ny)]
        mine = update(parts, mine, last)
        if not last:
            blocks = [mine] + [lax.ppermute(mine, "y", shifts[ny - d]) for d in range(1, ny)]
    final = exchange(mine.reshape(nz, held, width + EXTRA), "z")
    return final[..., :width], jnp.sum(final[..., width:].astype(jnp.float32), axis=-1)


def solution(mesh):
    fine = Mesh(mesh.devices.reshape(4, 2, 4, 4), ("x", "core", "z", "y"))
    point, cent = ("x", "core"), ("z", "y")
    return jax.shard_map(
        shards,
        mesh=fine,
        in_specs=(P(point + cent, None), P(point + cent), P(), P(point, cent, None)),
        out_specs=(P(point, cent, None), P(point, cent)),
        check_vma=False,
    )
```

```python
import functools

import jax
import jax.numpy as jnp
from jax import lax
from jax.experimental import pallas as pl
from jax.experimental.pallas import tpu as pltpu
from jax.sharding import Mesh, PartitionSpec as P

ITERS = 2
SCORE_SCALE = 0.25
PRIOR_WEIGHT = 1.0
EXTRA = 128
MARK = 1024.0
MARK_LIMIT = 512.0
GROUP = 256
SUB = 8
MIB = 1024 * 1024
VMEM = 60 * MIB
RING = 4
LINE_Z = 6
TILE = 8
AXES = ("x", "core", "z", "y")
SWAPPED = ((1, 0, 0), (3, 0, 0), (1, 3, 0), (3, 1, 0), (2, 0, 0))
DIRECT = ((1, 0, 3), (3, 0, 1), (0, 1, 3), (0, 3, 1))


def scatter_kernel(capacity, where, ids_ref, base_ref, points_ref, *refs):
    outs, (slots_v, slots_s, x, wide, placed, packed, in_sems, out_sems, slot_sem) = (
        refs[:-9],
        refs[-9:],
    )
    rows, width = points_ref.shape
    lanes = width // SUB
    parts = in_sems.shape[0]
    part = rows // parts
    loads = [
        pltpu.make_async_copy(
            points_ref.at[pl.ds(p * part, part)], x.at[pl.ds(p * part, part)], in_sems.at[p]
        )
        for p in range(parts)
    ]
    for load in loads:
        load.start()

    clusters = base_ref.shape[0]
    before = (
        lax.broadcasted_iota(jnp.int32, (GROUP, GROUP), 0)
        < lax.broadcasted_iota(jnp.int32, (GROUP, GROUP), 1)
    ).astype(jnp.float32).astype(jnp.bfloat16)
    table = lax.broadcasted_iota(jnp.int32, (clusters, GROUP), 0)
    base = base_ref[...].astype(jnp.float32)
    for g in range(rows // GROUP):
        span = pl.ds(g * GROUP, GROUP)
        hit = (table == ids_ref[:, span]).astype(jnp.float32)
        place = jnp.dot(hit.astype(jnp.bfloat16), before, preferred_element_type=jnp.float32)
        slot = jnp.sum(hit * (place + base), axis=0, keepdims=True).astype(jnp.int32)
        slots_v[:, span] = (slot // SUB) * (SUB * SUB) + slot % SUB
        base = base + jnp.sum(hit, axis=1, keepdims=True)
    to_scalars = pltpu.make_async_copy(slots_v, slots_s, slot_sem)
    to_scalars.start()

    def clear(i, _):
        placed[pl.ds(i * 256, 256)] = jnp.full((256, lanes), MARK, jnp.float32)
        return 0

    lax.fori_loop(0, placed.shape[0] // 256, clear, 0)

    def widen(i, _):
        two = x[pl.ds(i * 2 * SUB, 2 * SUB)].astype(jnp.float32)
        for h in range(2):
            for t in range(SUB):
                wide[pl.ds(((2 * i + h) * SUB + t) * SUB, SUB)] = two[
                    h * SUB : (h + 1) * SUB, t * lanes : (t + 1) * lanes
                ]
        return 0

    for p in range(parts):
        loads[p].wait()
        steps = part // (2 * SUB)
        lax.fori_loop(p * steps, (p + 1) * steps, widen, 0, unroll=2)
    to_scalars.wait()

    def move_rows(i, _):
        for r in range(2 * SUB):
            row = wide[pl.ds(i * 2 * SUB * SUB + r // SUB * SUB * SUB + r % SUB, SUB, stride=SUB)]
            placed[pl.ds(slots_s[0, i * 2 * SUB + r], SUB, stride=SUB)] = row
        return 0

    lax.fori_loop(0, rows // (2 * SUB), move_rows, 0)

    stores = []
    for n, (o, k) in enumerate(where):

        def narrow(i, _, n=n):
            first = n * capacity * SUB + i * 2 * SUB * SUB
            for t in range(SUB):
                low = placed[pl.ds(first + t * SUB, SUB)]
                high = placed[pl.ds(first + (SUB + t) * SUB, SUB)]
                packed[n, pl.ds(i * 2 * SUB, 2 * SUB), t * lanes : (t + 1) * lanes] = (
                    jnp.concatenate([low, high], axis=0).astype(jnp.bfloat16)
                )
            return 0

        lax.fori_loop(0, capacity // (2 * SUB), narrow, 0, unroll=2)
        stores.append(pltpu.make_async_copy(packed.at[n], outs[o].at[k], out_sems.at[n]))
        stores[-1].start()
    for store in stores:
        store.wait()


def scatter(cluster_ids, base, points, capacity, blocks):
    rows, width = points.shape
    where = [(o, k) for o, count in enumerate(blocks) for k in range(count)]
    any_space = pl.BlockSpec(memory_space=pl.ANY)
    whole = pl.BlockSpec(memory_space=pltpu.VMEM)
    lanes = width // SUB
    parts = 8
    return pl.pallas_call(
        functools.partial(scatter_kernel, capacity, where),
        in_specs=[whole, whole, any_space],
        out_specs=[any_space] * len(blocks),
        out_shape=[jax.ShapeDtypeStruct((n, capacity, width), jnp.bfloat16) for n in blocks],
        scratch_shapes=[
            pltpu.VMEM((1, rows), jnp.int32),
            pltpu.SMEM((1, rows), jnp.int32),
            pltpu.VMEM((rows, width), jnp.bfloat16),
            pltpu.VMEM((rows * SUB, lanes), jnp.float32),
            pltpu.VMEM((len(where) * capacity * SUB, lanes), jnp.float32),
            pltpu.VMEM((len(where), capacity, width), jnp.bfloat16),
            pltpu.SemaphoreType.DMA((parts,)),
            pltpu.SemaphoreType.DMA((len(where),)),
            pltpu.SemaphoreType.DMA,
        ],
        compiler_params=pltpu.CompilerParams(vmem_limit_bytes=VMEM),
        cost_estimate=pl.CostEstimate(
            flops=rows * width,
            bytes_accessed=8 * width * (rows + len(where) * capacity),
            transcendentals=0,
        ),
        name="scatter",
    )(cluster_ids.reshape(1, rows), base.reshape(-1, 1), points)


def sums_kernel(groups, counts, carried, finish, z_ref, *refs):
    blocks, refs = refs[:groups], refs[groups:]
    sources, refs = refs[: len(counts)], refs[len(counts) :]
    carry, refs = refs[: 2 * carried], refs[2 * carried :]
    outs, (aug, total, mass, bias, rows, sems) = refs[:-6], refs[-6:]
    held, width = blocks[0].shape
    cents = groups * held
    pieces = []
    for ref, count in zip(sources, counts):
        if count == LINE_Z:
            pieces += [
                (ref, c * RING + lax.rem(z_ref[0] + d, RING)) for c in range(2) for d in range(1, RING)
            ]
        else:
            pieces += [(ref, i) for i in range(count)]
    for n, (ref, i) in enumerate(pieces):
        pltpu.make_async_copy(ref.at[i], rows.at[n], sems.at[n]).start()

    for g in range(groups):
        mu = blocks[g][...]
        span = pl.ds(g * held, held)
        aug[span] = mu
        wide = mu.astype(jnp.float32)
        bias[span] = 0.5 * jnp.sum(wide * wide, axis=1, keepdims=True)
    unit = lax.broadcasted_iota(jnp.int32, (aug.shape[0] - cents, width), 1) == 0
    aug[cents:] = unit.astype(jnp.float32).astype(jnp.bfloat16)
    if carried:
        total[...] = carry[0][...]
        mass[...] = carry[1][...]
    else:
        total[...] = jnp.zeros_like(total)
        mass[...] = jnp.zeros_like(mass)

    def tile(t, _):
        for i in range(TILE):
            n = t * TILE + i
            pltpu.make_async_copy(sources[0].at[0], rows.at[n], sems.at[n]).wait()
        x = rows[pl.ds(t * TILE, TILE)].reshape(-1, width)
        raw = lax.dot_general(
            aug[...], x, (((1,), (1,)), ((), ())), preferred_element_type=jnp.float32
        )
        score = (raw[:cents] - bias[...]) * SCORE_SCALE
        present = (raw[cents : cents + 1] < MARK_LIMIT).astype(jnp.float32)
        e = jnp.exp(score - jnp.max(score, axis=0, keepdims=True))
        w = e * (present / jnp.sum(e, axis=0, keepdims=True))
        mass[...] += jnp.sum(w, axis=1, keepdims=True)
        total[...] += jnp.dot(w.astype(jnp.bfloat16), x, preferred_element_type=jnp.float32)
        return 0

    lax.fori_loop(0, len(pieces) // TILE, tile, 0)
    if not finish:
        outs[0][...] = total[...]
        outs[1][...] = mass[...]
        return
    lane = lax.broadcasted_iota(jnp.int32, (held, EXTRA), 1)
    for g in range(groups):
        span = pl.ds(g * held, held)
        outs[g][:, :width] = total[span].astype(jnp.bfloat16)
        outs[g][:, width:] = terms(mass[span], lane)


def cluster_sums(z, blocks, sources, counts, carry=(), finish=True):
    groups = len(blocks)
    held, width = blocks[0].shape
    capacity = sources[0].shape[1]
    cents, pieces = groups * held, sum(counts)
    assert pieces % TILE == 0
    whole = pl.BlockSpec(memory_space=pltpu.VMEM)
    if finish:
        shapes = [jax.ShapeDtypeStruct((held, width + EXTRA), jnp.bfloat16)] * groups
    else:
        shapes = [
            jax.ShapeDtypeStruct((cents, width), jnp.float32),
            jax.ShapeDtypeStruct((cents, 1), jnp.float32),
        ]
    count = pieces * capacity
    return pl.pallas_call(
        functools.partial(sums_kernel, groups, counts, 1 if carry else 0, finish),
        in_specs=[pl.BlockSpec(memory_space=pltpu.SMEM)]
        + [whole] * groups
        + [pl.BlockSpec(memory_space=pl.ANY)] * len(sources)
        + [whole] * len(carry),
        out_specs=[whole] * len(shapes),
        out_shape=shapes,
        scratch_shapes=[
            pltpu.VMEM((cents + 16, width), jnp.bfloat16),
            pltpu.VMEM((cents, width), jnp.float32),
            pltpu.VMEM((cents, 1), jnp.float32),
            pltpu.VMEM((cents, 1), jnp.float32),
            pltpu.VMEM((pieces, capacity, width), jnp.bfloat16),
            pltpu.SemaphoreType.DMA((pieces,)),
        ],
        compiler_params=pltpu.CompilerParams(vmem_limit_bytes=VMEM),
        cost_estimate=pl.CostEstimate(
            flops=4 * count * cents * width,
            bytes_accessed=2 * width * (count + 2 * cents),
            transcendentals=count * cents,
        ),
        name="cluster_sums",
    )(z.reshape(1), *blocks, *sources, *carry)


def terms(m, lane):
    hi = m.astype(jnp.bfloat16).astype(jnp.float32)
    mid = (m - hi).astype(jnp.bfloat16).astype(jnp.float32)
    low = m - hi - mid
    parts = jnp.where(lane == 0, hi, jnp.where(lane == 1, mid, jnp.where(lane == 2, low, 0.0)))
    return parts.astype(jnp.bfloat16)


def update_kernel(packed, count, *refs):
    parts, mu_ref, out_ref = refs[:count], refs[count], refs[count + 1]
    rows, width = mu_ref.shape
    total = parts[0][...].astype(jnp.float32)
    for s in range(1, count):
        total = total + parts[s][...].astype(jnp.float32)
    mass = jnp.sum(total[:, width:], axis=1, keepdims=True)
    mu = mu_ref[...].astype(jnp.float32)
    new = (total[:, :width] + PRIOR_WEIGHT * mu) / (mass + PRIOR_WEIGHT)
    out_ref[:, :width] = new.astype(jnp.bfloat16)
    if packed:
        out_ref[:, width:] = terms(mass, lax.broadcasted_iota(jnp.int32, (rows, EXTRA), 1))


def update(parts, mu, packed):
    rows, width = mu.shape
    return pl.pallas_call(
        functools.partial(update_kernel, packed, len(parts)),
        out_shape=jax.ShapeDtypeStruct((rows, width + (EXTRA if packed else 0)), jnp.bfloat16),
        compiler_params=pltpu.CompilerParams(vmem_limit_bytes=VMEM),
        cost_estimate=pl.CostEstimate(
            flops=len(parts) * rows * width,
            bytes_accessed=2 * (len(parts) + 2) * rows * width,
            transcendentals=0,
        ),
        name="update",
    )(*parts, mu)


def spread_kernel(in_ref, out_ref):
    for i in range(RING):
        for k in range(RING):
            out_ref[i * RING + k] = in_ref[(i - k) % RING]


def spread(centroids):
    return pl.pallas_call(
        spread_kernel,
        out_shape=jax.ShapeDtypeStruct((RING * RING,) + centroids.shape[1:], centroids.dtype),
        compiler_params=pltpu.CompilerParams(vmem_limit_bytes=VMEM),
        name="spread",
    )(centroids)


def finish_kernel(first_ref, *refs):
    parts, (new_ref, mass_ref) = refs[:RING], refs[RING:]
    width = new_ref.shape[2]
    ones = jnp.ones((8, EXTRA), jnp.bfloat16)
    for d in range(RING):
        j = lax.rem(first_ref[0] - d + RING, RING)
        new_ref[j] = parts[d][:, :width]
        mass = lax.dot_general(
            ones, parts[d][:, width:], (((1,), (1,)), ((), ())), preferred_element_type=jnp.float32
        )
        mass_ref[pl.ds(j, 1)] = mass[:1]


def finish(parts, first):
    rows, width = parts[0].shape
    whole = pl.BlockSpec(memory_space=pltpu.VMEM)
    return pl.pallas_call(
        finish_kernel,
        in_specs=[pl.BlockSpec(memory_space=pltpu.SMEM)] + [whole] * RING,
        out_specs=[whole] * 2,
        out_shape=[
            jax.ShapeDtypeStruct((RING, rows, width - EXTRA), jnp.bfloat16),
            jax.ShapeDtypeStruct((RING, rows), jnp.float32),
        ],
        compiler_params=pltpu.CompilerParams(vmem_limit_bytes=VMEM),
        name="finish",
    )(first.reshape(1), *parts)


def exchange(array, axis):
    return lax.all_to_all(array, axis, split_axis=0, concat_axis=0, tiled=True)


def number(x, core, z, y):
    return ((x % RING * 2 + core) * RING + z % RING) * RING + y % RING


def move(array, step):
    pairs = [
        (number(x, c, z, y), number(*step(x, c, z, y)))
        for x in range(RING)
        for c in range(2)
        for z in range(RING)
        for y in range(RING)
    ]
    return lax.ppermute(array, AXES, pairs)


def along(array, dx, dz, dy, flip=0):
    return move(array, lambda x, c, z, y: (x + dx, c ^ flip, z + dz, y + dy))


def first_slots(owner_slot, capacity, x, core, z, y):
    to_x, to_core, j = owner_slot // 8, owner_slot // 4 % 2, owner_slot % 4
    ra, rb = (to_x - x + y) % RING, (j - z + y) % RING
    block = 2 * RING + to_core * RING + (j + y) % RING
    block = jnp.where(ra == rb, to_core * RING + (y - ra) % RING, block)
    n = 4 * RING
    for dx, dz, dy in SWAPPED + DIRECT:
        here = (ra == (dx - dy) % RING) & (rb == (dz - dy) % RING)
        block = jnp.where(here, n + (to_core ^ core), block)
        n += 2
    return block * capacity


def shards(points, cluster_ids, owner_slot, centroids):
    rows, width = points.shape
    capacity = 2 * rows // owner_slot.shape[0]
    held = centroids.shape[1]
    x, core, z, y = (lax.axis_index(a) for a in AXES)

    gathered = exchange(spread(centroids), ("z", "y"))
    gathered = move(gathered, lambda x, c, z, y: (x + y, c, z, y))
    by_y = gathered.reshape(RING, RING, held, width).swapaxes(0, 1).reshape(RING, -1, width)
    blocks = [
        lax.dynamic_index_in_dim(by_y, (y + d) % RING, 0, keepdims=False) for d in range(RING)
    ]
    mine = blocks[0]

    line = 2 * RING
    to_y, to_z, *leaving = scatter(
        cluster_ids,
        first_slots(owner_slot, capacity, x, core, z, y),
        points,
        capacity,
        [line, line] + [2] * len(SWAPPED) + [1] * (2 * len(DIRECT)),
    )
    from_y = exchange(to_y, ("core", "y"))
    from_z = exchange(to_z, ("core", "z"))
    came = [along(leaving[i], *route) for i, route in enumerate(SWAPPED)]
    other = jnp.stack([c[1] for c in came])
    swapped = move(other, lambda x, c, z, y: (x, 1 - c, z, y))
    straight = []
    for i, route in enumerate(DIRECT):
        first = len(SWAPPED) + 2 * i
        straight.append(along(leaving[first], *route))
        straight.append(along(leaving[first + 1], *route, 1))

    arrays = [from_y] + came + [swapped, from_z] + straight
    counts = [line] + [1] * len(SWAPPED) + [len(SWAPPED), LINE_Z] + [1] * len(straight)
    carry = cluster_sums(z, blocks, [from_y], [line], finish=False)
    for iteration in range(ITERS):
        last = iteration == ITERS - 1
        if iteration == 0:
            sums = cluster_sums(z, blocks, arrays[1:], counts[1:], carry)
        else:
            sums = cluster_sums(z, blocks, arrays, counts)
        parts = [sums[0]] + [along(sums[d], d, d, d) for d in range(1, RING)]
        mine = update(parts, mine, last)
        if not last:
            blocks = [mine] + [along(mine, -d, -d, -d) for d in range(1, RING)]
    by_z = mine.reshape(RING, held, width + EXTRA)
    leaving = [lax.dynamic_index_in_dim(by_z, (z + d) % RING, 0, keepdims=False) for d in range(RING)]
    came = [
        move(leaving[d], functools.partial(lambda d, x, c, z, y: (x - y, c, z + d, y), d))
        for d in range(RING)
    ]
    new, mass = finish(came, (z - y) % RING)
    return new, mass


def solution(mesh):
    fine = Mesh(mesh.devices.reshape(RING, 2, RING, RING), AXES)
    point, cent = AXES[:2], AXES[2:]
    return jax.shard_map(
        shards,
        mesh=fine,
        in_specs=(P(point + cent, None), P(point + cent), P(), P(point, cent, None)),
        out_specs=(P(point, cent, None), P(point, cent)),
        check_vma=False,
    )
```

```python
import functools

import jax
import jax.numpy as jnp
from jax import lax
from jax.experimental import pallas as pl
from jax.experimental.pallas import tpu as pltpu
from jax.sharding import Mesh, PartitionSpec as P

ITERS = 2
SCORE_SCALE = 0.25
PRIOR_WEIGHT = 1.0
EXTRA = 128
MARK = 1024.0
MARK_LIMIT = 512.0
GROUP = 256
SUB = 8
MIB = 1024 * 1024
VMEM = 60 * MIB
RING = 4
TILE = 8
AXES = ("x", "core", "z", "y")


def scatter_kernel(capacity, where, ids_ref, base_ref, points_ref, *refs):
    outs, (slots_v, slots_s, x, wide, placed, packed, in_sems, out_sems, slot_sem) = (
        refs[:-9],
        refs[-9:],
    )
    rows, width = points_ref.shape
    lanes = width // SUB
    parts = in_sems.shape[0]
    part = rows // parts
    loads = [
        pltpu.make_async_copy(
            points_ref.at[pl.ds(p * part, part)], x.at[pl.ds(p * part, part)], in_sems.at[p]
        )
        for p in range(parts)
    ]
    for load in loads:
        load.start()

    clusters = base_ref.shape[0]
    before = (
        lax.broadcasted_iota(jnp.int32, (GROUP, GROUP), 0)
        < lax.broadcasted_iota(jnp.int32, (GROUP, GROUP), 1)
    ).astype(jnp.float32).astype(jnp.bfloat16)
    table = lax.broadcasted_iota(jnp.int32, (clusters, GROUP), 0)
    base = base_ref[...].astype(jnp.float32)
    for g in range(rows // GROUP):
        span = pl.ds(g * GROUP, GROUP)
        hit = (table == ids_ref[:, span]).astype(jnp.float32)
        place = jnp.dot(hit.astype(jnp.bfloat16), before, preferred_element_type=jnp.float32)
        slot = jnp.sum(hit * (place + base), axis=0, keepdims=True).astype(jnp.int32)
        slots_v[:, span] = (slot // SUB) * (SUB * SUB) + slot % SUB
        base = base + jnp.sum(hit, axis=1, keepdims=True)
    to_scalars = pltpu.make_async_copy(slots_v, slots_s, slot_sem)
    to_scalars.start()

    def clear(i, _):
        placed[pl.ds(i * 256, 256)] = jnp.full((256, lanes), MARK, jnp.float32)
        return 0

    lax.fori_loop(0, placed.shape[0] // 256, clear, 0)

    def widen(i, _):
        two = x[pl.ds(i * 2 * SUB, 2 * SUB)].astype(jnp.float32)
        for h in range(2):
            for t in range(SUB):
                wide[pl.ds(((2 * i + h) * SUB + t) * SUB, SUB)] = two[
                    h * SUB : (h + 1) * SUB, t * lanes : (t + 1) * lanes
                ]
        return 0

    for p in range(parts):
        loads[p].wait()
        steps = part // (2 * SUB)
        lax.fori_loop(p * steps, (p + 1) * steps, widen, 0, unroll=2)
    to_scalars.wait()

    def move_rows(i, _):
        for r in range(2 * SUB):
            row = wide[pl.ds(i * 2 * SUB * SUB + r // SUB * SUB * SUB + r % SUB, SUB, stride=SUB)]
            placed[pl.ds(slots_s[0, i * 2 * SUB + r], SUB, stride=SUB)] = row
        return 0

    lax.fori_loop(0, rows // (2 * SUB), move_rows, 0)

    stores = []
    for n, (o, k) in enumerate(where):

        def narrow(i, _, n=n):
            first = n * capacity * SUB + i * 2 * SUB * SUB
            for t in range(SUB):
                low = placed[pl.ds(first + t * SUB, SUB)]
                high = placed[pl.ds(first + (SUB + t) * SUB, SUB)]
                packed[n, pl.ds(i * 2 * SUB, 2 * SUB), t * lanes : (t + 1) * lanes] = (
                    jnp.concatenate([low, high], axis=0).astype(jnp.bfloat16)
                )
            return 0

        lax.fori_loop(0, capacity // (2 * SUB), narrow, 0, unroll=2)
        stores.append(pltpu.make_async_copy(packed.at[n], outs[o].at[k], out_sems.at[n]))
        stores[-1].start()
    for store in stores:
        store.wait()


def scatter(cluster_ids, base, points, capacity, blocks):
    rows, width = points.shape
    where = [(o, k) for o, count in enumerate(blocks) for k in range(count)]
    any_space = pl.BlockSpec(memory_space=pl.ANY)
    whole = pl.BlockSpec(memory_space=pltpu.VMEM)
    lanes = width // SUB
    parts = 8
    return pl.pallas_call(
        functools.partial(scatter_kernel, capacity, where),
        in_specs=[whole, whole, any_space],
        out_specs=[any_space] * len(blocks),
        out_shape=[jax.ShapeDtypeStruct((n, capacity, width), jnp.bfloat16) for n in blocks],
        scratch_shapes=[
            pltpu.VMEM((1, rows), jnp.int32),
            pltpu.SMEM((1, rows), jnp.int32),
            pltpu.VMEM((rows, width), jnp.bfloat16),
            pltpu.VMEM((rows * SUB, lanes), jnp.float32),
            pltpu.VMEM((len(where) * capacity * SUB, lanes), jnp.float32),
            pltpu.VMEM((len(where), capacity, width), jnp.bfloat16),
            pltpu.SemaphoreType.DMA((parts,)),
            pltpu.SemaphoreType.DMA((len(where),)),
            pltpu.SemaphoreType.DMA,
        ],
        compiler_params=pltpu.CompilerParams(vmem_limit_bytes=VMEM),
        cost_estimate=pl.CostEstimate(
            flops=rows * width,
            bytes_accessed=8 * width * (rows + len(where) * capacity),
            transcendentals=0,
        ),
        name="scatter",
    )(cluster_ids.reshape(1, rows), base.reshape(-1, 1), points)


def sums_kernel(groups, counts, carried, last, y_ref, *refs):
    blocks, refs = refs[:groups], refs[groups:]
    sources, refs = refs[: len(counts)], refs[len(counts) :]
    carry, refs = refs[: 2 * carried], refs[2 * carried :]
    outs, (aug, total, mass, bias, rows, sems) = refs[:-6], refs[-6:]
    held, width = blocks[0].shape
    cents = groups * held
    pieces = [(ref, i) for ref, count in zip(sources, counts) for i in range(count)]
    for n, (ref, i) in enumerate(pieces):
        pltpu.make_async_copy(ref.at[i], rows.at[n], sems.at[n]).start()

    for g in range(groups):
        mu = blocks[g][...]
        span = pl.ds(g * held, held)
        aug[span] = mu
        wide = mu.astype(jnp.float32)
        bias[span] = 0.5 * jnp.sum(wide * wide, axis=1, keepdims=True)
    unit = lax.broadcasted_iota(jnp.int32, (aug.shape[0] - cents, width), 1) == 0
    aug[cents:] = unit.astype(jnp.float32).astype(jnp.bfloat16)
    if carried:
        total[...] = carry[0][...]
        mass[...] = carry[1][...]
    else:
        total[...] = jnp.zeros_like(total)
        mass[...] = jnp.zeros_like(mass)
    if last:
        total[:held] += PRIOR_WEIGHT * blocks[0][...].astype(jnp.float32)

    def tile(t, _):
        for i in range(TILE):
            n = t * TILE + i
            pltpu.make_async_copy(sources[0].at[0], rows.at[n], sems.at[n]).wait()
        x = rows[pl.ds(t * TILE, TILE)].reshape(-1, width)
        raw = lax.dot_general(
            aug[...], x, (((1,), (1,)), ((), ())), preferred_element_type=jnp.float32
        )
        score = (raw[:cents] - bias[...]) * SCORE_SCALE
        present = (raw[cents : cents + 1] < MARK_LIMIT).astype(jnp.float32)
        e = jnp.exp(score - jnp.max(score, axis=0, keepdims=True))
        w = e * (present / jnp.sum(e, axis=0, keepdims=True))
        mass[...] += jnp.sum(w, axis=1, keepdims=True)
        total[...] += jnp.dot(w.astype(jnp.bfloat16), x, preferred_element_type=jnp.float32)
        return 0

    lax.fori_loop(0, len(pieces) // TILE, tile, 0)
    if not last and len(outs) == 2:
        outs[0][...] = total[...]
        outs[1][...] = mass[...]
        return
    if not last:
        lane = lax.broadcasted_iota(jnp.int32, (held, EXTRA), 1)
        for g in range(groups):
            span = pl.ds(g * held, held)
            outs[g][:, :width] = total[span].astype(jnp.bfloat16)
            outs[g][:, width:] = terms(mass[span], lane)
        return
    shard = held // RING
    lane = lax.broadcasted_iota(jnp.int32, (shard, EXTRA), 1)
    for g in range(groups):
        to_y = lax.rem(y_ref[0] + g, RING)
        for z in range(RING):
            span = pl.ds(g * held + z * shard, shard)
            holder = z * RING + to_y
            outs[0][holder, :, :width] = total[span].astype(jnp.bfloat16)
            outs[0][holder, :, width:] = terms(mass[span], lane)


def cluster_sums(y, blocks, sources, counts, carry=(), partial=False, last=False):
    groups = len(blocks)
    held, width = blocks[0].shape
    capacity = sources[0].shape[1]
    cents, pieces = groups * held, sum(counts)
    assert pieces % TILE == 0
    whole = pl.BlockSpec(memory_space=pltpu.VMEM)
    if partial:
        shapes = [
            jax.ShapeDtypeStruct((cents, width), jnp.float32),
            jax.ShapeDtypeStruct((cents, 1), jnp.float32),
        ]
    elif last:
        shape = (groups * RING, held // RING, width + EXTRA)
        shapes = [jax.ShapeDtypeStruct(shape, jnp.bfloat16)]
    else:
        shapes = [jax.ShapeDtypeStruct((held, width + EXTRA), jnp.bfloat16)] * groups
    count = pieces * capacity
    return pl.pallas_call(
        functools.partial(sums_kernel, groups, counts, 1 if carry else 0, last),
        in_specs=[pl.BlockSpec(memory_space=pltpu.SMEM)]
        + [whole] * groups
        + [pl.BlockSpec(memory_space=pl.ANY)] * len(sources)
        + [whole] * len(carry),
        out_specs=[whole] * len(shapes),
        out_shape=shapes,
        scratch_shapes=[
            pltpu.VMEM((cents + 16, width), jnp.bfloat16),
            pltpu.VMEM((cents, width), jnp.float32),
            pltpu.VMEM((cents, 1), jnp.float32),
            pltpu.VMEM((cents, 1), jnp.float32),
            pltpu.VMEM((pieces, capacity, width), jnp.bfloat16),
            pltpu.SemaphoreType.DMA((pieces,)),
        ],
        compiler_params=pltpu.CompilerParams(vmem_limit_bytes=VMEM),
        cost_estimate=pl.CostEstimate(
            flops=4 * count * cents * width,
            bytes_accessed=2 * width * (count + 2 * cents),
            transcendentals=count * cents,
        ),
        name="cluster_sums",
    )(y.reshape(1), *blocks, *sources, *carry)


def terms(m, lane):
    hi = m.astype(jnp.bfloat16).astype(jnp.float32)
    mid = (m - hi).astype(jnp.bfloat16).astype(jnp.float32)
    low = m - hi - mid
    parts = jnp.where(lane == 0, hi, jnp.where(lane == 1, mid, jnp.where(lane == 2, low, 0.0)))
    return parts.astype(jnp.bfloat16)


def update_kernel(*refs):
    parts, mu_ref, out_ref = refs[:-2], refs[-2], refs[-1]
    width = mu_ref.shape[1]
    total = parts[0][...].astype(jnp.float32)
    for part in parts[1:]:
        total = total + part[...].astype(jnp.float32)
    mass = jnp.sum(total[:, width:], axis=1, keepdims=True)
    mu = mu_ref[...].astype(jnp.float32)
    new = (total[:, :width] + PRIOR_WEIGHT * mu) / (mass + PRIOR_WEIGHT)
    out_ref[...] = new.astype(jnp.bfloat16)


def update(parts, mu):
    rows, width = mu.shape
    return pl.pallas_call(
        update_kernel,
        out_shape=jax.ShapeDtypeStruct((rows, width), jnp.bfloat16),
        compiler_params=pltpu.CompilerParams(vmem_limit_bytes=VMEM),
        cost_estimate=pl.CostEstimate(
            flops=len(parts) * rows * width,
            bytes_accessed=2 * (len(parts) + 2) * rows * width,
            transcendentals=0,
        ),
        name="update",
    )(*parts, mu)


def assemble_kernel(z_ref, *refs):
    parts, out_ref = refs[:-1], refs[-1]
    shard = parts[0].shape[0]
    for d, part in enumerate(parts):
        start = pl.multiple_of(lax.rem(z_ref[0] - d + RING, RING) * shard, shard)
        out_ref[pl.ds(start, shard)] = part[...]


def assemble(z, parts):
    rows, width = parts[0].shape
    whole = pl.BlockSpec(memory_space=pltpu.VMEM)
    return pl.pallas_call(
        assemble_kernel,
        in_specs=[pl.BlockSpec(memory_space=pltpu.SMEM)] + [whole] * len(parts),
        out_specs=whole,
        out_shape=jax.ShapeDtypeStruct((len(parts) * rows, width), jnp.bfloat16),
        compiler_params=pltpu.CompilerParams(vmem_limit_bytes=VMEM),
        name="assemble",
    )(z.reshape(1), *parts)


def finish_kernel(parts_ref, new_ref, mass_ref):
    width = new_ref.shape[2]
    ones = jnp.ones((8, EXTRA), jnp.bfloat16)
    for j in range(RING):
        total, mass = 0.0, 0.0
        for y in range(RING):
            part = parts_ref[j * RING + y]
            total = total + part.astype(jnp.float32)
            mass = mass + lax.dot_general(
                ones, part[:, width:], (((1,), (1,)), ((), ())), preferred_element_type=jnp.float32
            )
        column = jnp.sum(total[:, width:], axis=1, keepdims=True)
        new_ref[j] = (total[:, :width] / (column + PRIOR_WEIGHT)).astype(jnp.bfloat16)
        mass_ref[pl.ds(j, 1)] = mass[:1]


def finish(parts):
    _, rows, width = parts.shape
    return pl.pallas_call(
        finish_kernel,
        out_shape=[
            jax.ShapeDtypeStruct((RING, rows, width - EXTRA), jnp.bfloat16),
            jax.ShapeDtypeStruct((RING, rows), jnp.float32),
        ],
        compiler_params=pltpu.CompilerParams(vmem_limit_bytes=VMEM),
        name="finish",
    )(parts)


def exchange(array, axis):
    return lax.all_to_all(array, axis, split_axis=0, concat_axis=0, tiled=True)


def shift(array, axis, d):
    return lax.ppermute(array, axis, [(i, (i + d) % RING) for i in range(RING)])


def shards(points, cluster_ids, owner_slot, centroids):
    rows, width = points.shape
    clusters = owner_slot.shape[0]
    capacity = 2 * rows // clusters
    z, y = lax.axis_index("z"), lax.axis_index("y")

    (leaving,) = scatter(cluster_ids, owner_slot * capacity, points, capacity, [clusters])
    arrived = exchange(leaving, ("x", "core", "z"))

    own = [lax.dynamic_index_in_dim(centroids, (z + d) % RING, 0, keepdims=False) for d in range(RING)]
    own = own[:1] + [shift(own[d], "z", d) for d in range(1, RING)]
    mine = assemble(z, own)
    for iteration in range(ITERS):
        blocks = [mine] + [shift(mine, "y", -d) for d in range(1, RING)]
        last = iteration == ITERS - 1
        sums = cluster_sums(y, blocks, [arrived], [clusters], last=last)
        if not last:
            parts = [sums[0]] + [shift(sums[d], "y", d) for d in range(1, RING)]
            mine = update(parts, mine)
    new, mass = finish(exchange(sums[0], ("z", "y")))
    return new, mass


def solution(mesh):
    fine = Mesh(mesh.devices.reshape(RING, 2, RING, RING), AXES)
    point, cent = AXES[:2], AXES[2:]
    return jax.shard_map(
        shards,
        mesh=fine,
        in_specs=(P(point + cent, None), P(point + cent), P(), P(point, cent, None)),
        out_specs=(P(point, cent, None), P(point, cent)),
        check_vma=False,
    )
```

```python
import functools

import jax
import jax.numpy as jnp
from jax import lax
from jax.experimental import pallas as pl
from jax.experimental.pallas import tpu as pltpu
from jax.sharding import Mesh, PartitionSpec as P

SCORE_SCALE = 0.25
PRIOR_WEIGHT = 1.0
EXTRA = 128
MARK = 1024.0
MARK_LIMIT = 512.0
GROUP = 256
SUB = 8
MIB = 1024 * 1024
VMEM = 60 * MIB
RING = 4
TILE = 8
AXES = ("x", "core", "z", "y")


def scatter_kernel(capacity, where, ids_ref, owner_ref, points_ref, *refs):
    outs, (slots_v, slots_s, x, wide, placed, packed, in_sems, out_sems, slot_sem) = (
        refs[:-9],
        refs[-9:],
    )
    rows, width = points_ref.shape
    lanes = width // SUB
    parts = in_sems.shape[0]
    part = rows // parts
    loads = [
        pltpu.make_async_copy(
            points_ref.at[pl.ds(p * part, part)], x.at[pl.ds(p * part, part)], in_sems.at[p]
        )
        for p in range(parts)
    ]
    for load in loads:
        load.start()

    clusters = owner_ref.shape[1]
    before = (
        lax.broadcasted_iota(jnp.int32, (GROUP, GROUP), 0)
        < lax.broadcasted_iota(jnp.int32, (GROUP, GROUP), 1)
    ).astype(jnp.float32).astype(jnp.bfloat16)
    table = lax.broadcasted_iota(jnp.int32, (clusters, GROUP), 0)
    same = lax.broadcasted_iota(jnp.int32, (clusters, clusters), 0) == (
        lax.broadcasted_iota(jnp.int32, (clusters, clusters), 1)
    )
    owners = jnp.broadcast_to(owner_ref[...], (clusters, clusters)).astype(jnp.float32)
    base = jnp.sum(jnp.where(same, owners, 0.0), axis=1, keepdims=True) * capacity
    for g in range(rows // GROUP):
        span = pl.ds(g * GROUP, GROUP)
        hit = (table == ids_ref[:, span]).astype(jnp.float32)
        place = jnp.dot(hit.astype(jnp.bfloat16), before, preferred_element_type=jnp.float32)
        slot = jnp.sum(hit * (place + base), axis=0, keepdims=True).astype(jnp.int32)
        slots_v[:, span] = (slot // SUB) * (SUB * SUB) + slot % SUB
        base = base + jnp.sum(hit, axis=1, keepdims=True)
    to_scalars = pltpu.make_async_copy(slots_v, slots_s, slot_sem)
    to_scalars.start()

    def clear(i, _):
        placed[pl.ds(i * 256, 256)] = jnp.full((256, lanes), MARK, jnp.float32)
        return 0

    lax.fori_loop(0, placed.shape[0] // 256, clear, 0)

    def widen(i, _):
        two = x[pl.ds(i * 2 * SUB, 2 * SUB)].astype(jnp.float32)
        for h in range(2):
            for t in range(SUB):
                wide[pl.ds(((2 * i + h) * SUB + t) * SUB, SUB)] = two[
                    h * SUB : (h + 1) * SUB, t * lanes : (t + 1) * lanes
                ]
        return 0

    for p in range(parts):
        loads[p].wait()
        steps = part // (2 * SUB)
        lax.fori_loop(p * steps, (p + 1) * steps, widen, 0, unroll=2)
    to_scalars.wait()

    def move_rows(i, _):
        for r in range(2 * SUB):
            row = wide[pl.ds(i * 2 * SUB * SUB + r // SUB * SUB * SUB + r % SUB, SUB, stride=SUB)]
            placed[pl.ds(slots_s[0, i * 2 * SUB + r], SUB, stride=SUB)] = row
        return 0

    lax.fori_loop(0, rows // (2 * SUB), move_rows, 0)

    stores = []
    for n, (o, k) in enumerate(where):

        def narrow(i, _, n=n):
            first = n * capacity * SUB + i * 2 * SUB * SUB
            for t in range(SUB):
                low = placed[pl.ds(first + t * SUB, SUB)]
                high = placed[pl.ds(first + (SUB + t) * SUB, SUB)]
                packed[n, pl.ds(i * 2 * SUB, 2 * SUB), t * lanes : (t + 1) * lanes] = (
                    jnp.concatenate([low, high], axis=0).astype(jnp.bfloat16)
                )
            return 0

        lax.fori_loop(0, capacity // (2 * SUB), narrow, 0, unroll=2)
        stores.append(pltpu.make_async_copy(packed.at[n], outs[o].at[k], out_sems.at[n]))
        stores[-1].start()
    for store in stores:
        store.wait()


def scatter(cluster_ids, owner_slot, points, capacity, blocks):
    rows, width = points.shape
    where = [(o, k) for o, count in enumerate(blocks) for k in range(count)]
    any_space = pl.BlockSpec(memory_space=pl.ANY)
    whole = pl.BlockSpec(memory_space=pltpu.VMEM)
    lanes = width // SUB
    parts = 8
    return pl.pallas_call(
        functools.partial(scatter_kernel, capacity, where),
        in_specs=[whole, whole, any_space],
        out_specs=[any_space] * len(blocks),
        out_shape=[jax.ShapeDtypeStruct((n, capacity, width), jnp.bfloat16) for n in blocks],
        scratch_shapes=[
            pltpu.VMEM((1, rows), jnp.int32),
            pltpu.SMEM((1, rows), jnp.int32),
            pltpu.VMEM((rows, width), jnp.bfloat16),
            pltpu.VMEM((rows * SUB, lanes), jnp.float32),
            pltpu.VMEM((len(where) * capacity * SUB, lanes), jnp.float32),
            pltpu.VMEM((len(where), capacity, width), jnp.bfloat16),
            pltpu.SemaphoreType.DMA((parts,)),
            pltpu.SemaphoreType.DMA((len(where),)),
            pltpu.SemaphoreType.DMA,
        ],
        compiler_params=pltpu.CompilerParams(vmem_limit_bytes=VMEM),
        cost_estimate=pl.CostEstimate(
            flops=rows * width,
            bytes_accessed=8 * width * (rows + len(where) * capacity),
            transcendentals=0,
        ),
        name="scatter",
    )(cluster_ids.reshape(1, rows), owner_slot.reshape(1, -1), points)


def sums_kernel(groups, last, y_ref, source, *refs):
    if last:
        blocks, refs = refs[:groups], refs[groups:]
    else:
        blocks, refs = [refs[0].at[g] for g in range(groups)], refs[1:]
    if last:
        rows, outs, (aug, total, mass, bias) = source, refs[:1], refs[1:]
    else:
        rows, outs, (aug, total, mass, bias, sems) = refs[0], refs[1:-5], refs[-5:]
    held, width = blocks[0].shape[-2:]
    cents = groups * held
    pieces = rows.shape[0]
    if not last:
        for n in range(pieces):
            pltpu.make_async_copy(source.at[n], rows.at[n], sems.at[n]).start()

    for g in range(groups):
        mu = blocks[g][...]
        span = pl.ds(g * held, held)
        aug[span] = mu
        wide = mu.astype(jnp.float32)
        bias[span] = 0.5 * jnp.sum(wide * wide, axis=1, keepdims=True)
    unit = lax.broadcasted_iota(jnp.int32, (aug.shape[0] - cents, width), 1) == 0
    aug[cents:] = unit.astype(jnp.float32).astype(jnp.bfloat16)
    total[...] = jnp.zeros_like(total)
    mass[...] = jnp.zeros_like(mass)
    if last:
        total[:held] += PRIOR_WEIGHT * blocks[0][...].astype(jnp.float32)

    def tile(t, _):
        if not last:
            for i in range(TILE):
                n = t * TILE + i
                pltpu.make_async_copy(source.at[n], rows.at[n], sems.at[n]).wait()
        x = rows[pl.ds(t * TILE, TILE)].reshape(-1, width)
        raw = lax.dot_general(
            aug[...], x, (((1,), (1,)), ((), ())), preferred_element_type=jnp.float32
        )
        score = (raw[:cents] - bias[...]) * SCORE_SCALE
        present = (raw[cents : cents + 1] < MARK_LIMIT).astype(jnp.float32)
        e = jnp.exp(score - jnp.max(score, axis=0, keepdims=True))
        w = e * (present / jnp.sum(e, axis=0, keepdims=True))
        mass[...] += jnp.sum(w, axis=1, keepdims=True)
        total[...] += jnp.dot(w.astype(jnp.bfloat16), x, preferred_element_type=jnp.float32)
        return 0

    lax.fori_loop(0, pieces // TILE, tile, 0)
    if not last:
        lane = lax.broadcasted_iota(jnp.int32, (held, EXTRA), 1)
        for g in range(groups):
            span = pl.ds(g * held, held)
            outs[g][:, :width] = total[span].astype(jnp.bfloat16)
            outs[g][:, width:] = terms(mass[span], lane)
        return
    shard = held // RING
    lane = lax.broadcasted_iota(jnp.int32, (shard, EXTRA), 1)
    for g in range(groups):
        to_y = lax.rem(y_ref[0] + g, RING)
        for z in range(RING):
            span = pl.ds(g * held + z * shard, shard)
            holder = z * RING + to_y
            outs[0][holder, :, :width] = total[span].astype(jnp.bfloat16)
            outs[0][holder, :, width:] = terms(mass[span], lane)


def cluster_sums(y, blocks, rows, last):
    groups = RING
    held, width = blocks[0].shape[-2:]
    pieces, capacity, _ = rows.shape
    cents = groups * held
    assert pieces % TILE == 0
    whole = pl.BlockSpec(memory_space=pltpu.VMEM)
    if last:
        shape = (groups * RING, held // RING, width + EXTRA)
        shapes = [jax.ShapeDtypeStruct(shape, jnp.bfloat16)]
        sems = []
    else:
        shapes = [pltpu.VMEM(rows.shape, rows.dtype)]
        shapes += [jax.ShapeDtypeStruct((held, width + EXTRA), jnp.bfloat16)] * groups
        sems = [pltpu.SemaphoreType.DMA((pieces,))]
    count = pieces * capacity
    return pl.pallas_call(
        functools.partial(sums_kernel, groups, last),
        in_specs=[
            pl.BlockSpec(memory_space=pltpu.SMEM),
            whole if last else pl.BlockSpec(memory_space=pl.ANY),
        ]
        + [whole] * len(blocks),
        out_specs=[whole] * len(shapes),
        out_shape=shapes,
        scratch_shapes=[
            pltpu.VMEM((cents + 16, width), jnp.bfloat16),
            pltpu.VMEM((cents, width), jnp.float32),
            pltpu.VMEM((cents, 1), jnp.float32),
            pltpu.VMEM((cents, 1), jnp.float32),
        ]
        + sems,
        compiler_params=pltpu.CompilerParams(vmem_limit_bytes=32 * MIB),
        cost_estimate=pl.CostEstimate(
            flops=4 * count * cents * width,
            bytes_accessed=2 * width * (count + 2 * cents),
            transcendentals=count * cents,
        ),
        name="cluster_sums",
    )(y.reshape(1), rows, *blocks)


def terms(m, lane):
    hi = m.astype(jnp.bfloat16).astype(jnp.float32)
    mid = (m - hi).astype(jnp.bfloat16).astype(jnp.float32)
    low = m - hi - mid
    parts = jnp.where(lane == 0, hi, jnp.where(lane == 1, mid, jnp.where(lane == 2, low, 0.0)))
    return parts.astype(jnp.bfloat16)


def update_kernel(*refs):
    parts, mu_ref, out_ref = refs[:-2], refs[-2], refs[-1]
    width = mu_ref.shape[-1]
    total = parts[0][...].astype(jnp.float32)
    for part in parts[1:]:
        total = total + part[...].astype(jnp.float32)
    mass = jnp.sum(total[:, width:], axis=1, keepdims=True)
    mu = mu_ref[0].astype(jnp.float32)
    new = (total[:, :width] + PRIOR_WEIGHT * mu) / (mass + PRIOR_WEIGHT)
    out_ref[...] = new.astype(jnp.bfloat16)


def update(parts, mu):
    rows, width = mu.shape[-2:]
    return pl.pallas_call(
        update_kernel,
        out_shape=jax.ShapeDtypeStruct((rows, width), jnp.bfloat16),
        compiler_params=pltpu.CompilerParams(vmem_limit_bytes=16 * MIB),
        cost_estimate=pl.CostEstimate(
            flops=len(parts) * rows * width,
            bytes_accessed=2 * (len(parts) + 2) * rows * width,
            transcendentals=0,
        ),
        name="update",
    )(*parts, mu)


def choose_kernel(z_ref, *refs):
    parts, outs = refs[:RING], refs[RING:]
    for d, out_ref in enumerate(outs):
        j = lax.rem(z_ref[0] + d, RING)
        for g, part in enumerate(parts):
            out_ref[g] = part[j]


def choose(z, parts):
    whole = pl.BlockSpec(memory_space=pltpu.VMEM)
    return pl.pallas_call(
        choose_kernel,
        in_specs=[pl.BlockSpec(memory_space=pltpu.SMEM)] + [whole] * RING,
        out_specs=[whole] * RING,
        out_shape=[jax.ShapeDtypeStruct(parts[0].shape, parts[0].dtype)] * RING,
        compiler_params=pltpu.CompilerParams(vmem_limit_bytes=16 * MIB),
        name="choose",
    )(z.reshape(1), *parts)


def assemble_kernel(z_ref, *refs):
    parts, out_ref = refs[:-1], refs[-1]
    groups, shard, _ = parts[0].shape
    for d, part in enumerate(parts):
        start = pl.multiple_of(lax.rem(z_ref[0] - d + RING, RING) * shard, shard)
        for g in range(groups):
            out_ref[g, pl.ds(start, shard)] = part[g]


def assemble(z, parts):
    groups, rows, width = parts[0].shape
    whole = pl.BlockSpec(memory_space=pltpu.VMEM)
    return pl.pallas_call(
        assemble_kernel,
        in_specs=[pl.BlockSpec(memory_space=pltpu.SMEM)] + [whole] * len(parts),
        out_specs=whole,
        out_shape=jax.ShapeDtypeStruct((groups, len(parts) * rows, width), jnp.bfloat16),
        compiler_params=pltpu.CompilerParams(vmem_limit_bytes=16 * MIB),
        name="assemble",
    )(z.reshape(1), *parts)


def finish_kernel(parts_ref, new_ref, mass_ref):
    width = new_ref.shape[2]
    ones = jnp.ones((8, EXTRA), jnp.bfloat16)
    for j in range(RING):
        total, mass = 0.0, 0.0
        for y in range(RING):
            part = parts_ref[j * RING + y]
            total = total + part.astype(jnp.float32)
            mass = mass + lax.dot_general(
                ones, part[:, width:], (((1,), (1,)), ((), ())), preferred_element_type=jnp.float32
            )
        column = jnp.sum(total[:, width:], axis=1, keepdims=True)
        new_ref[j] = (total[:, :width] / (column + PRIOR_WEIGHT)).astype(jnp.bfloat16)
        mass_ref[pl.ds(j, 1)] = mass[:1]


def finish(parts):
    _, rows, width = parts.shape
    return pl.pallas_call(
        finish_kernel,
        out_shape=[
            jax.ShapeDtypeStruct((RING, rows, width - EXTRA), jnp.bfloat16),
            jax.ShapeDtypeStruct((RING, rows), jnp.float32),
        ],
        compiler_params=pltpu.CompilerParams(vmem_limit_bytes=16 * MIB),
        name="finish",
    )(parts)


def exchange(array, axis):
    return lax.all_to_all(array, axis, split_axis=0, concat_axis=0, tiled=True)


def shift(array, axis, d):
    return lax.ppermute(array, axis, [(i, (i + d) % RING) for i in range(RING)])


def shards(points, cluster_ids, owner_slot, centroids):
    rows, width = points.shape
    clusters = owner_slot.shape[0]
    capacity = 2 * rows // clusters
    z, y = lax.axis_index("z"), lax.axis_index("y")

    (leaving,) = scatter(cluster_ids, owner_slot, points, capacity, [clusters])
    arrived = exchange(leaving, ("x", "core", "z"))

    by_y = [centroids] + [shift(centroids, "y", -d) for d in range(1, RING)]
    to_z = list(choose(z, by_y))
    block = assemble(z, to_z[:1] + [shift(to_z[d], "z", d) for d in range(1, RING)])
    arrived, *sums = cluster_sums(y, [block], arrived, False)
    parts = [sums[0]] + [shift(sums[d], "y", d) for d in range(1, RING)]
    mine = update(parts, block)
    blocks = [mine] + [shift(mine, "y", -d) for d in range(1, RING)]
    (sums,) = cluster_sums(y, blocks, arrived, True)
    new, mass = finish(exchange(sums, ("z", "y")))
    return new, mass


def solution(mesh):
    fine = Mesh(mesh.devices.reshape(RING, 2, RING, RING), AXES)
    point, cent = AXES[:2], AXES[2:]
    return jax.shard_map(
        shards,
        mesh=fine,
        in_specs=(P(point + cent, None), P(point + cent), P(), P(point, cent, None)),
        out_specs=(P(point, cent, None), P(point, cent)),
        check_vma=False,
    )
```

```python
import functools

import jax
import jax.numpy as jnp
from jax import lax
from jax.experimental import pallas as pl
from jax.experimental.pallas import tpu as pltpu
from jax.sharding import Mesh, PartitionSpec as P

SCORE_SCALE = 0.25
PRIOR_WEIGHT = 1.0
EXTRA = 128
MARK = 1024.0
MARK_LIMIT = 512.0
GROUP = 256
SUB = 8
MIB = 1024 * 1024
VMEM = 60 * MIB
RING = 4
TILE = 8
AXES = ("x", "core", "z", "y")


def scatter_kernel(capacity, where, ids_ref, owner_ref, points_ref, *refs):
    outs, (slots_v, slots_s, x, wide, placed, packed, in_sems, out_sems, slot_sem) = (
        refs[:-9],
        refs[-9:],
    )
    rows, width = points_ref.shape
    lanes = width // SUB
    parts = in_sems.shape[0]
    part = rows // parts
    loads = [
        pltpu.make_async_copy(
            points_ref.at[pl.ds(p * part, part)], x.at[pl.ds(p * part, part)], in_sems.at[p]
        )
        for p in range(parts)
    ]
    for load in loads:
        load.start()

    clusters = owner_ref.shape[1]
    before = (
        lax.broadcasted_iota(jnp.int32, (GROUP, GROUP), 0)
        < lax.broadcasted_iota(jnp.int32, (GROUP, GROUP), 1)
    ).astype(jnp.float32).astype(jnp.bfloat16)
    table = lax.broadcasted_iota(jnp.int32, (clusters, GROUP), 0)
    same = lax.broadcasted_iota(jnp.int32, (clusters, clusters), 0) == (
        lax.broadcasted_iota(jnp.int32, (clusters, clusters), 1)
    )
    owner = owner_ref[...]
    order = (owner // 8) * 1 + (owner // 4 % 2) * 4 + (owner % 4) * 8
    owners = jnp.broadcast_to(order, (clusters, clusters)).astype(jnp.float32)
    base = jnp.sum(jnp.where(same, owners, 0.0), axis=1, keepdims=True) * capacity
    for g in range(rows // GROUP):
        span = pl.ds(g * GROUP, GROUP)
        hit = (table == ids_ref[:, span]).astype(jnp.float32)
        place = jnp.dot(hit.astype(jnp.bfloat16), before, preferred_element_type=jnp.float32)
        slot = jnp.sum(hit * (place + base), axis=0, keepdims=True).astype(jnp.int32)
        slots_v[:, span] = (slot // SUB) * (SUB * SUB) + slot % SUB
        base = base + jnp.sum(hit, axis=1, keepdims=True)
    to_scalars = pltpu.make_async_copy(slots_v, slots_s, slot_sem)
    to_scalars.start()

    def clear(i, _):
        placed[pl.ds(i * 256, 256)] = jnp.full((256, lanes), MARK, jnp.float32)
        return 0

    lax.fori_loop(0, placed.shape[0] // 256, clear, 0)

    def widen(i, _):
        two = x[pl.ds(i * 2 * SUB, 2 * SUB)].astype(jnp.float32)
        for h in range(2):
            for t in range(SUB):
                wide[pl.ds(((2 * i + h) * SUB + t) * SUB, SUB)] = two[
                    h * SUB : (h + 1) * SUB, t * lanes : (t + 1) * lanes
                ]
        return 0

    for p in range(parts):
        loads[p].wait()
        steps = part // (2 * SUB)
        lax.fori_loop(p * steps, (p + 1) * steps, widen, 0, unroll=2)
    to_scalars.wait()

    def move_rows(i, _):
        for r in range(2 * SUB):
            row = wide[pl.ds(i * 2 * SUB * SUB + r // SUB * SUB * SUB + r % SUB, SUB, stride=SUB)]
            placed[pl.ds(slots_s[0, i * 2 * SUB + r], SUB, stride=SUB)] = row
        return 0

    lax.fori_loop(0, rows // (2 * SUB), move_rows, 0, unroll=2)

    stores = []
    for n, (o, k) in enumerate(where):

        def narrow(i, _, n=n):
            first = n * capacity * SUB + i * 2 * SUB * SUB
            for t in range(SUB):
                low = placed[pl.ds(first + t * SUB, SUB)]
                high = placed[pl.ds(first + (SUB + t) * SUB, SUB)]
                packed[n, pl.ds(i * 2 * SUB, 2 * SUB), t * lanes : (t + 1) * lanes] = (
                    jnp.concatenate([low, high], axis=0).astype(jnp.bfloat16)
                )
            return 0

        lax.fori_loop(0, capacity // (2 * SUB), narrow, 0, unroll=2)
        stores.append(pltpu.make_async_copy(packed.at[n], outs[o].at[k], out_sems.at[n]))
        stores[-1].start()
    for store in stores:
        store.wait()


def scatter(cluster_ids, owner_slot, points, capacity, blocks):
    rows, width = points.shape
    where = [(o, k) for o, count in enumerate(blocks) for k in range(count)]
    any_space = pl.BlockSpec(memory_space=pl.ANY)
    whole = pl.BlockSpec(memory_space=pltpu.VMEM)
    lanes = width // SUB
    parts = 8
    return pl.pallas_call(
        functools.partial(scatter_kernel, capacity, where),
        in_specs=[whole, whole, any_space],
        out_specs=[any_space] * len(blocks),
        out_shape=[jax.ShapeDtypeStruct((n, capacity, width), jnp.bfloat16) for n in blocks],
        scratch_shapes=[
            pltpu.VMEM((1, rows), jnp.int32),
            pltpu.SMEM((1, rows), jnp.int32),
            pltpu.VMEM((rows, width), jnp.bfloat16),
            pltpu.VMEM((rows * SUB, lanes), jnp.float32),
            pltpu.VMEM((len(where) * capacity * SUB, lanes), jnp.float32),
            pltpu.VMEM((len(where), capacity, width), jnp.bfloat16),
            pltpu.SemaphoreType.DMA((parts,)),
            pltpu.SemaphoreType.DMA((len(where),)),
            pltpu.SemaphoreType.DMA,
        ],
        compiler_params=pltpu.CompilerParams(vmem_limit_bytes=VMEM),
        cost_estimate=pl.CostEstimate(
            flops=rows * width,
            bytes_accessed=8 * width * (rows + len(where) * capacity),
            transcendentals=0,
        ),
        name="scatter",
    )(cluster_ids.reshape(1, rows), owner_slot.reshape(1, -1), points)


def sums_kernel(groups, last, y_ref, source, *refs):
    if last:
        blocks, refs = refs[:groups], refs[groups:]
    else:
        blocks, refs = [refs[0].at[g] for g in range(groups)], refs[1:]
    if last:
        rows, outs, (aug, total, mass, bias) = source, refs[:1], refs[1:]
    else:
        rows, outs, (aug, total, mass, bias, sems) = refs[0], refs[1:-5], refs[-5:]
    held, width = blocks[0].shape[-2:]
    cents = groups * held
    pieces = rows.shape[0]
    if not last:
        for n in range(pieces):
            pltpu.make_async_copy(source.at[n], rows.at[n], sems.at[n]).start()

    for g in range(groups):
        mu = blocks[g][...]
        span = pl.ds(g * held, held)
        aug[span] = mu
        wide = mu.astype(jnp.float32)
        bias[span] = 0.5 * jnp.sum(wide * wide, axis=1, keepdims=True)
    unit = lax.broadcasted_iota(jnp.int32, (aug.shape[0] - cents, width), 1) == 0
    aug[cents:] = unit.astype(jnp.float32).astype(jnp.bfloat16)
    total[...] = jnp.zeros_like(total)
    mass[...] = jnp.zeros_like(mass)
    if last:
        total[:held] += PRIOR_WEIGHT * blocks[0][...].astype(jnp.float32)

    def load(t):
        if not last:
            for n in range(t * TILE, (t + 1) * TILE):
                pltpu.make_async_copy(source.at[n], rows.at[n], sems.at[n]).wait()
        return rows[t * TILE : (t + 1) * TILE].reshape(-1, width)

    def product(x):
        return lax.dot_general(
            aug[...], x, (((1,), (1,)), ((), ())), preferred_element_type=jnp.float32
        )

    x = load(0)
    raw = product(x)
    for t in range(pieces // TILE):
        now, members = raw, x
        if (t + 1) * TILE < pieces:
            x = load(t + 1)
            raw = product(x)
        score = (now[:cents] - bias[...]) * SCORE_SCALE
        present = (now[cents : cents + 1] < MARK_LIMIT).astype(jnp.float32)
        e = jnp.exp(score - jnp.max(score, axis=0, keepdims=True))
        w = e * (present / jnp.sum(e, axis=0, keepdims=True))
        mass[...] += jnp.sum(w, axis=1, keepdims=True)
        total[...] += jnp.dot(
            w.astype(jnp.bfloat16), members, preferred_element_type=jnp.float32
        )
    if not last:
        lane = lax.broadcasted_iota(jnp.int32, (held, EXTRA), 1)
        for g in range(groups):
            span = pl.ds(g * held, held)
            outs[g][:, :width] = total[span].astype(jnp.bfloat16)
            outs[g][:, width:] = terms(mass[span], lane)
        return
    shard = held // RING
    lane = lax.broadcasted_iota(jnp.int32, (shard, EXTRA), 1)
    for g in range(groups):
        to_y = lax.rem(y_ref[0] + g, RING)
        for z in range(RING):
            span = pl.ds(g * held + z * shard, shard)
            holder = z * RING + to_y
            outs[0][holder, :, :width] = total[span].astype(jnp.bfloat16)
            outs[0][holder, :, width:] = terms(mass[span], lane)


def cluster_sums(y, blocks, rows, last):
    groups = RING
    held, width = blocks[0].shape[-2:]
    pieces, capacity, _ = rows.shape
    cents = groups * held
    assert pieces % TILE == 0
    whole = pl.BlockSpec(memory_space=pltpu.VMEM)
    if last:
        shape = (groups * RING, held // RING, width + EXTRA)
        shapes = [jax.ShapeDtypeStruct(shape, jnp.bfloat16)]
        sems = []
    else:
        shapes = [pltpu.VMEM(rows.shape, rows.dtype)]
        shapes += [jax.ShapeDtypeStruct((held, width + EXTRA), jnp.bfloat16)] * groups
        sems = [pltpu.SemaphoreType.DMA((pieces,))]
    count = pieces * capacity
    return pl.pallas_call(
        functools.partial(sums_kernel, groups, last),
        in_specs=[
            pl.BlockSpec(memory_space=pltpu.SMEM),
            whole if last else pl.BlockSpec(memory_space=pl.ANY),
        ]
        + [whole] * len(blocks),
        out_specs=[whole] * len(shapes),
        out_shape=shapes,
        scratch_shapes=[
            pltpu.VMEM((cents + 16, width), jnp.bfloat16),
            pltpu.VMEM((cents, width), jnp.float32),
            pltpu.VMEM((cents, 1), jnp.float32),
            pltpu.VMEM((cents, 1), jnp.float32),
        ]
        + sems,
        compiler_params=pltpu.CompilerParams(vmem_limit_bytes=32 * MIB),
        cost_estimate=pl.CostEstimate(
            flops=4 * count * cents * width,
            bytes_accessed=2 * width * (count + 2 * cents),
            transcendentals=count * cents,
        ),
        name="cluster_sums",
    )(y.reshape(1), rows, *blocks)


def terms(m, lane):
    hi = m.astype(jnp.bfloat16).astype(jnp.float32)
    mid = (m - hi).astype(jnp.bfloat16).astype(jnp.float32)
    low = m - hi - mid
    parts = jnp.where(lane == 0, hi, jnp.where(lane == 1, mid, jnp.where(lane == 2, low, 0.0)))
    return parts.astype(jnp.bfloat16)


def update_kernel(*refs):
    parts, mu_ref, out_ref = refs[:-2], refs[-2], refs[-1]
    width = mu_ref.shape[-1]
    total = parts[0][...].astype(jnp.float32)
    for part in parts[1:]:
        total = total + part[...].astype(jnp.float32)
    mass = jnp.sum(total[:, width:], axis=1, keepdims=True)
    mu = mu_ref[0].astype(jnp.float32)
    new = (total[:, :width] + PRIOR_WEIGHT * mu) / (mass + PRIOR_WEIGHT)
    out_ref[...] = new.astype(jnp.bfloat16)


def update(parts, mu):
    rows, width = mu.shape[-2:]
    return pl.pallas_call(
        update_kernel,
        out_shape=jax.ShapeDtypeStruct((rows, width), jnp.bfloat16),
        compiler_params=pltpu.CompilerParams(vmem_limit_bytes=16 * MIB),
        cost_estimate=pl.CostEstimate(
            flops=len(parts) * rows * width,
            bytes_accessed=2 * (len(parts) + 2) * rows * width,
            transcendentals=0,
        ),
        name="update",
    )(*parts, mu)


def choose_kernel(z_ref, *refs):
    parts, outs = refs[:RING], refs[RING:]
    for d, out_ref in enumerate(outs):
        j = lax.rem(z_ref[0] + d, RING)
        for g, part in enumerate(parts):
            out_ref[g] = part[j]


def choose(z, parts):
    whole = pl.BlockSpec(memory_space=pltpu.VMEM)
    return pl.pallas_call(
        choose_kernel,
        in_specs=[pl.BlockSpec(memory_space=pltpu.SMEM)] + [whole] * RING,
        out_specs=[whole] * RING,
        out_shape=[jax.ShapeDtypeStruct(parts[0].shape, parts[0].dtype)] * RING,
        compiler_params=pltpu.CompilerParams(vmem_limit_bytes=16 * MIB),
        name="choose",
    )(z.reshape(1), *parts)


def assemble_kernel(z_ref, *refs):
    parts, out_ref = refs[:-1], refs[-1]
    groups, shard, _ = parts[0].shape
    for d, part in enumerate(parts):
        start = pl.multiple_of(lax.rem(z_ref[0] - d + RING, RING) * shard, shard)
        for g in range(groups):
            out_ref[g, pl.ds(start, shard)] = part[g]


def assemble(z, parts):
    groups, rows, width = parts[0].shape
    whole = pl.BlockSpec(memory_space=pltpu.VMEM)
    return pl.pallas_call(
        assemble_kernel,
        in_specs=[pl.BlockSpec(memory_space=pltpu.SMEM)] + [whole] * len(parts),
        out_specs=whole,
        out_shape=jax.ShapeDtypeStruct((groups, len(parts) * rows, width), jnp.bfloat16),
        compiler_params=pltpu.CompilerParams(vmem_limit_bytes=16 * MIB),
        name="assemble",
    )(z.reshape(1), *parts)


def finish_kernel(parts_ref, new_ref, mass_ref):
    width = new_ref.shape[2]
    ones = jnp.ones((8, EXTRA), jnp.bfloat16)
    for j in range(RING):
        total, mass = 0.0, 0.0
        for y in range(RING):
            part = parts_ref[j * RING + y]
            total = total + part.astype(jnp.float32)
            mass = mass + lax.dot_general(
                ones, part[:, width:], (((1,), (1,)), ((), ())), preferred_element_type=jnp.float32
            )
        column = jnp.sum(total[:, width:], axis=1, keepdims=True)
        new_ref[j] = (total[:, :width] / (column + PRIOR_WEIGHT)).astype(jnp.bfloat16)
        mass_ref[pl.ds(j, 1)] = mass[:1]


def finish(parts):
    _, rows, width = parts.shape
    return pl.pallas_call(
        finish_kernel,
        out_shape=[
            jax.ShapeDtypeStruct((RING, rows, width - EXTRA), jnp.bfloat16),
            jax.ShapeDtypeStruct((RING, rows), jnp.float32),
        ],
        compiler_params=pltpu.CompilerParams(vmem_limit_bytes=16 * MIB),
        name="finish",
    )(parts)


def exchange(array, axis):
    return lax.all_to_all(array, axis, split_axis=0, concat_axis=0, tiled=True)


def shift(array, axis, d):
    return lax.ppermute(array, axis, [(i, (i + d) % RING) for i in range(RING)])


def shards(points, cluster_ids, owner_slot, centroids):
    rows, width = points.shape
    clusters = owner_slot.shape[0]
    capacity = 2 * rows // clusters
    z, y = lax.axis_index("z"), lax.axis_index("y")

    (leaving,) = scatter(cluster_ids, owner_slot, points, capacity, [clusters])
    arrived = exchange(leaving, ("z", "core", "x"))

    by_y = [centroids] + [shift(centroids, "y", -d) for d in range(1, RING)]
    to_z = list(choose(z, by_y))
    block = assemble(z, to_z[:1] + [shift(to_z[d], "z", d) for d in range(1, RING)])
    arrived, *sums = cluster_sums(y, [block], arrived, False)
    parts = [sums[0]] + [shift(sums[d], "y", d) for d in (2, 1, 3)]
    mine = update(parts, block)
    near, back, far = (shift(mine, "y", -d) for d in (1, 3, 2))
    blocks = [mine, near, far, back]
    (sums,) = cluster_sums(y, blocks, arrived, True)
    new, mass = finish(exchange(sums, ("z", "y")))
    return new, mass


def solution(mesh):
    fine = Mesh(mesh.devices.reshape(RING, 2, RING, RING), AXES)
    point, cent = AXES[:2], AXES[2:]
    return jax.shard_map(
        shards,
        mesh=fine,
        in_specs=(P(point + cent, None), P(point + cent), P(), P(point, cent, None)),
        out_specs=(P(point, cent, None), P(point, cent)),
        check_vma=False,
    )
```

```python
import functools

import jax
import jax.numpy as jnp
from jax import lax
from jax.experimental import pallas as pl
from jax.experimental.pallas import tpu as pltpu
from jax.sharding import Mesh, PartitionSpec as P

SCORE_SCALE = 0.25
PRIOR_WEIGHT = 1.0
EXTRA = 128
MARK = 1024.0
MARK_LIMIT = 512.0
GROUP = 256
SUB = 8
MIB = 1024 * 1024
VMEM = 60 * MIB
RING = 4
TILE = 8
AXES = ("x", "core", "z", "y")


def scatter_kernel(capacity, where, ids_ref, owner_ref, points_ref, *refs):
    outs, (slots_v, slots_s, x, wide, placed, packed, in_sems, out_sems, slot_sem) = (
        refs[:-9],
        refs[-9:],
    )
    rows, width = points_ref.shape
    lanes = width // SUB
    parts = in_sems.shape[0]
    part = rows // parts
    loads = [
        pltpu.make_async_copy(
            points_ref.at[pl.ds(p * part, part)], x.at[pl.ds(p * part, part)], in_sems.at[p]
        )
        for p in range(parts)
    ]
    for load in loads:
        load.start()

    clusters = owner_ref.shape[1]
    before = (
        lax.broadcasted_iota(jnp.int32, (GROUP, GROUP), 0)
        < lax.broadcasted_iota(jnp.int32, (GROUP, GROUP), 1)
    ).astype(jnp.float32).astype(jnp.bfloat16)
    table = lax.broadcasted_iota(jnp.int32, (clusters, GROUP), 0)
    same = lax.broadcasted_iota(jnp.int32, (clusters, clusters), 0) == (
        lax.broadcasted_iota(jnp.int32, (clusters, clusters), 1)
    )
    owner = owner_ref[...]
    order = (owner // 8) * 1 + (owner // 4 % 2) * 4 + (owner % 4) * 8
    owners = jnp.broadcast_to(order, (clusters, clusters)).astype(jnp.float32)
    base = jnp.sum(jnp.where(same, owners, 0.0), axis=1, keepdims=True) * capacity
    for g in range(rows // GROUP):
        span = pl.ds(g * GROUP, GROUP)
        hit = (table == ids_ref[:, span]).astype(jnp.float32)
        place = jnp.dot(hit.astype(jnp.bfloat16), before, preferred_element_type=jnp.float32)
        slot = jnp.sum(hit * (place + base), axis=0, keepdims=True).astype(jnp.int32)
        slots_v[:, span] = (slot // SUB) * (SUB * SUB) + slot % SUB
        base = base + jnp.sum(hit, axis=1, keepdims=True)
    to_scalars = pltpu.make_async_copy(slots_v, slots_s, slot_sem)
    to_scalars.start()

    def clear(i, _):
        placed[pl.ds(i * 256, 256)] = jnp.full((256, lanes), MARK, jnp.float32)
        return 0

    lax.fori_loop(0, placed.shape[0] // 256, clear, 0)

    def widen(i, _):
        two = x[pl.ds(i * 2 * SUB, 2 * SUB)].astype(jnp.float32)
        for h in range(2):
            for t in range(SUB):
                wide[pl.ds(((2 * i + h) * SUB + t) * SUB, SUB)] = two[
                    h * SUB : (h + 1) * SUB, t * lanes : (t + 1) * lanes
                ]
        return 0

    for p in range(parts):
        loads[p].wait()
        steps = part // (2 * SUB)
        lax.fori_loop(p * steps, (p + 1) * steps, widen, 0, unroll=2)
    to_scalars.wait()

    def move_rows(i, _):
        for r in range(2 * SUB):
            row = wide[pl.ds(i * 2 * SUB * SUB + r // SUB * SUB * SUB + r % SUB, SUB, stride=SUB)]
            placed[pl.ds(slots_s[0, i * 2 * SUB + r], SUB, stride=SUB)] = row
        return 0

    lax.fori_loop(0, rows // (2 * SUB), move_rows, 0, unroll=2)

    stores = []
    for n, (o, k) in enumerate(where):

        def narrow(i, _, n=n):
            first = n * capacity * SUB + i * 2 * SUB * SUB
            for t in range(SUB):
                low = placed[pl.ds(first + t * SUB, SUB)]
                high = placed[pl.ds(first + (SUB + t) * SUB, SUB)]
                packed[n, pl.ds(i * 2 * SUB, 2 * SUB), t * lanes : (t + 1) * lanes] = (
                    jnp.concatenate([low, high], axis=0).astype(jnp.bfloat16)
                )
            return 0

        lax.fori_loop(0, capacity // (2 * SUB), narrow, 0, unroll=2)
        stores.append(pltpu.make_async_copy(packed.at[n], outs[o].at[k], out_sems.at[n]))
        stores[-1].start()
    for store in stores:
        store.wait()


def scatter(cluster_ids, owner_slot, points, capacity, blocks):
    rows, width = points.shape
    where = [(o, k) for o, count in enumerate(blocks) for k in range(count)]
    any_space = pl.BlockSpec(memory_space=pl.ANY)
    whole = pl.BlockSpec(memory_space=pltpu.VMEM)
    lanes = width // SUB
    parts = 8
    return pl.pallas_call(
        functools.partial(scatter_kernel, capacity, where),
        in_specs=[whole, whole, any_space],
        out_specs=[any_space] * len(blocks),
        out_shape=[jax.ShapeDtypeStruct((n, capacity, width), jnp.bfloat16) for n in blocks],
        scratch_shapes=[
            pltpu.VMEM((1, rows), jnp.int32),
            pltpu.SMEM((1, rows), jnp.int32),
            pltpu.VMEM((rows, width), jnp.bfloat16),
            pltpu.VMEM((rows * SUB, lanes), jnp.float32),
            pltpu.VMEM((len(where) * capacity * SUB, lanes), jnp.float32),
            pltpu.VMEM((len(where), capacity, width), jnp.bfloat16),
            pltpu.SemaphoreType.DMA((parts,)),
            pltpu.SemaphoreType.DMA((len(where),)),
            pltpu.SemaphoreType.DMA,
        ],
        compiler_params=pltpu.CompilerParams(vmem_limit_bytes=VMEM),
        cost_estimate=pl.CostEstimate(
            flops=rows * width,
            bytes_accessed=8 * width * (rows + len(where) * capacity),
            transcendentals=0,
        ),
        name="scatter",
    )(cluster_ids.reshape(1, rows), owner_slot.reshape(1, -1), points)


def sums_kernel(groups, last, y_ref, source, *refs):
    if last:
        blocks, refs = refs[:groups], refs[groups:]
    else:
        blocks, refs = [refs[0].at[g] for g in range(groups)], refs[1:]
    if last:
        rows, outs, (aug, total, mass, bias) = source, refs[:1], refs[1:]
    else:
        rows, outs, (aug, total, mass, bias, sems) = refs[0], refs[1:-5], refs[-5:]
    held, width = blocks[0].shape[-2:]
    cents = groups * held
    pieces = rows.shape[0]
    tile = TILE // 2 if last else TILE
    if not last:
        for n in range(pieces):
            pltpu.make_async_copy(source.at[n], rows.at[n], sems.at[n]).start()

    for g in range(groups):
        mu = blocks[g][...]
        span = pl.ds(g * held, held)
        aug[span] = mu
        wide = mu.astype(jnp.float32)
        bias[span] = 0.5 * jnp.sum(wide * wide, axis=1, keepdims=True)
    unit = lax.broadcasted_iota(jnp.int32, (aug.shape[0] - cents, width), 1) == 0
    aug[cents:] = unit.astype(jnp.float32).astype(jnp.bfloat16)
    total[...] = jnp.zeros_like(total)
    mass[...] = jnp.zeros_like(mass)
    if last:
        total[:held] += PRIOR_WEIGHT * blocks[0][...].astype(jnp.float32)

    def load(t):
        if not last:
            for n in range(t * tile, (t + 1) * tile):
                pltpu.make_async_copy(source.at[n], rows.at[n], sems.at[n]).wait()
        return rows[t * tile : (t + 1) * tile].reshape(-1, width)

    def product(x):
        return lax.dot_general(
            aug[...], x, (((1,), (1,)), ((), ())), preferred_element_type=jnp.float32
        )

    x = load(0)
    raw = product(x)
    for t in range(pieces // tile):
        now, members = raw, x
        if (t + 1) * tile < pieces:
            x = load(t + 1)
            raw = product(x)
        score = (now[:cents] - bias[...]) * SCORE_SCALE
        present = (now[cents : cents + 1] < MARK_LIMIT).astype(jnp.float32)
        e = jnp.exp(score - jnp.max(score, axis=0, keepdims=True))
        w = e * (present / jnp.sum(e, axis=0, keepdims=True))
        mass[...] += jnp.sum(w, axis=1, keepdims=True)
        total[...] += jnp.dot(
            w.astype(jnp.bfloat16), members, preferred_element_type=jnp.float32
        )
    if not last:
        lane = lax.broadcasted_iota(jnp.int32, (held, EXTRA), 1)
        for g in range(groups):
            span = pl.ds(g * held, held)
            outs[g][:, :width] = total[span].astype(jnp.bfloat16)
            outs[g][:, width:] = terms(mass[span], lane)
        return
    shard = held // RING
    lane = lax.broadcasted_iota(jnp.int32, (shard, EXTRA), 1)
    for g in range(groups):
        to_y = lax.rem(y_ref[0] + g, RING)
        for z in range(RING):
            span = pl.ds(g * held + z * shard, shard)
            holder = to_y * RING + z
            outs[0][holder, :, :width] = total[span].astype(jnp.bfloat16)
            outs[0][holder, :, width:] = terms(mass[span], lane)


def cluster_sums(y, blocks, rows, last):
    groups = RING
    held, width = blocks[0].shape[-2:]
    pieces, capacity, _ = rows.shape
    cents = groups * held
    assert pieces % TILE == 0
    whole = pl.BlockSpec(memory_space=pltpu.VMEM)
    if last:
        shape = (groups * RING, held // RING, width + EXTRA)
        shapes = [jax.ShapeDtypeStruct(shape, jnp.bfloat16)]
        sems = []
    else:
        shapes = [pltpu.VMEM(rows.shape, rows.dtype)]
        shapes += [jax.ShapeDtypeStruct((held, width + EXTRA), jnp.bfloat16)] * groups
        sems = [pltpu.SemaphoreType.DMA((pieces,))]
    count = pieces * capacity
    return pl.pallas_call(
        functools.partial(sums_kernel, groups, last),
        in_specs=[
            pl.BlockSpec(memory_space=pltpu.SMEM),
            whole if last else pl.BlockSpec(memory_space=pl.ANY),
        ]
        + [whole] * len(blocks),
        out_specs=[whole] * len(shapes),
        out_shape=shapes,
        scratch_shapes=[
            pltpu.VMEM((cents + 16, width), jnp.bfloat16),
            pltpu.VMEM((cents, width), jnp.float32),
            pltpu.VMEM((cents, 1), jnp.float32),
            pltpu.VMEM((cents, 1), jnp.float32),
        ]
        + sems,
        compiler_params=pltpu.CompilerParams(vmem_limit_bytes=32 * MIB),
        cost_estimate=pl.CostEstimate(
            flops=4 * count * cents * width,
            bytes_accessed=2 * width * (count + 2 * cents),
            transcendentals=count * cents,
        ),
        name="cluster_sums",
    )(y.reshape(1), rows, *blocks)


def terms(m, lane):
    hi = m.astype(jnp.bfloat16).astype(jnp.float32)
    mid = (m - hi).astype(jnp.bfloat16).astype(jnp.float32)
    low = m - hi - mid
    parts = jnp.where(lane == 0, hi, jnp.where(lane == 1, mid, jnp.where(lane == 2, low, 0.0)))
    return parts.astype(jnp.bfloat16)


def update_kernel(*refs):
    parts, mu_ref, out_ref = refs[:-2], refs[-2], refs[-1]
    width = mu_ref.shape[-1]
    total = parts[0][...].astype(jnp.float32)
    for part in parts[1:]:
        total = total + part[...].astype(jnp.float32)
    mass = jnp.sum(total[:, width:], axis=1, keepdims=True)
    mu = mu_ref[0].astype(jnp.float32)
    new = (total[:, :width] + PRIOR_WEIGHT * mu) / (mass + PRIOR_WEIGHT)
    out_ref[...] = new.astype(jnp.bfloat16)


def update(parts, mu):
    rows, width = mu.shape[-2:]
    return pl.pallas_call(
        update_kernel,
        out_shape=jax.ShapeDtypeStruct((rows, width), jnp.bfloat16),
        compiler_params=pltpu.CompilerParams(vmem_limit_bytes=16 * MIB),
        cost_estimate=pl.CostEstimate(
            flops=len(parts) * rows * width,
            bytes_accessed=2 * (len(parts) + 2) * rows * width,
            transcendentals=0,
        ),
        name="update",
    )(*parts, mu)


def choose_kernel(z_ref, *refs):
    parts, outs = refs[:RING], refs[RING:]
    for d, out_ref in enumerate(outs):
        j = lax.rem(z_ref[0] + d, RING)
        for g, part in enumerate(parts):
            out_ref[g] = part[j]


def choose(z, parts):
    whole = pl.BlockSpec(memory_space=pltpu.VMEM)
    return pl.pallas_call(
        choose_kernel,
        in_specs=[pl.BlockSpec(memory_space=pltpu.SMEM)] + [whole] * RING,
        out_specs=[whole] * RING,
        out_shape=[jax.ShapeDtypeStruct(parts[0].shape, parts[0].dtype)] * RING,
        compiler_params=pltpu.CompilerParams(vmem_limit_bytes=16 * MIB),
        name="choose",
    )(z.reshape(1), *parts)


def assemble_kernel(z_ref, *refs):
    parts, out_ref = refs[:-1], refs[-1]
    groups, shard, _ = parts[0].shape
    for d, part in enumerate(parts):
        start = pl.multiple_of(lax.rem(z_ref[0] - d + RING, RING) * shard, shard)
        for g in range(groups):
            out_ref[g, pl.ds(start, shard)] = part[g]


def assemble(z, parts):
    groups, rows, width = parts[0].shape
    whole = pl.BlockSpec(memory_space=pltpu.VMEM)
    return pl.pallas_call(
        assemble_kernel,
        in_specs=[pl.BlockSpec(memory_space=pltpu.SMEM)] + [whole] * len(parts),
        out_specs=whole,
        out_shape=jax.ShapeDtypeStruct((groups, len(parts) * rows, width), jnp.bfloat16),
        compiler_params=pltpu.CompilerParams(vmem_limit_bytes=16 * MIB),
        name="assemble",
    )(z.reshape(1), *parts)


def finish_kernel(parts_ref, new_ref, mass_ref):
    width = new_ref.shape[2]
    ones = jnp.ones((8, EXTRA), jnp.bfloat16)
    for j in range(RING):
        total, mass = 0.0, 0.0
        for y in range(RING):
            part = parts_ref[y * RING + j]
            total = total + part.astype(jnp.float32)
            mass = mass + lax.dot_general(
                ones, part[:, width:], (((1,), (1,)), ((), ())), preferred_element_type=jnp.float32
            )
        column = jnp.sum(total[:, width:], axis=1, keepdims=True)
        new_ref[j] = (total[:, :width] / (column + PRIOR_WEIGHT)).astype(jnp.bfloat16)
        mass_ref[pl.ds(j, 1)] = mass[:1]


def finish(parts):
    _, rows, width = parts.shape
    return pl.pallas_call(
        finish_kernel,
        out_shape=[
            jax.ShapeDtypeStruct((RING, rows, width - EXTRA), jnp.bfloat16),
            jax.ShapeDtypeStruct((RING, rows), jnp.float32),
        ],
        compiler_params=pltpu.CompilerParams(vmem_limit_bytes=16 * MIB),
        name="finish",
    )(parts)


def exchange(array, axis):
    return lax.all_to_all(array, axis, split_axis=0, concat_axis=0, tiled=True)


def shift(array, axis, d):
    return lax.ppermute(array, axis, [(i, (i + d) % RING) for i in range(RING)])


def shards(points, cluster_ids, owner_slot, centroids):
    rows, width = points.shape
    clusters = owner_slot.shape[0]
    capacity = 2 * rows // clusters
    z, y = lax.axis_index("z"), lax.axis_index("y")

    (leaving,) = scatter(cluster_ids, owner_slot, points, capacity, [clusters])
    arrived = exchange(leaving, ("z", "core", "x"))

    by_y = [centroids] + [shift(centroids, "y", -d) for d in range(1, RING)]
    to_z = list(choose(z, by_y))
    block = assemble(z, to_z[:1] + [shift(to_z[d], "z", d) for d in range(1, RING)])
    arrived, *sums = cluster_sums(y, [block], arrived, False)
    parts = [sums[0]] + [shift(sums[d], "y", d) for d in (2, 1, 3)]
    mine = update(parts, block)
    near, back, far = (shift(mine, "y", -d) for d in (1, 3, 2))
    blocks = [mine, near, far, back]
    (sums,) = cluster_sums(y, blocks, arrived, True)
    new, mass = finish(exchange(sums, ("y", "z")))
    return new, mass


def solution(mesh):
    fine = Mesh(mesh.devices.reshape(RING, 2, RING, RING), AXES)
    point, cent = AXES[:2], AXES[2:]
    return jax.shard_map(
        shards,
        mesh=fine,
        in_specs=(P(point + cent, None), P(point + cent), P(), P(point, cent, None)),
        out_specs=(P(point, cent, None), P(point, cent)),
        check_vma=False,
    )
```
